32 devices in a mesh: grp: 4 (over x, core), dev: 8 (over z, y).
Axes of the slice: x: 2, y: 2, z: 4, core: 2. Of those that a mesh axis runs over, the one named last changes fastest.
Arguments:
- node_latent: bfloat16 [32, 128, 256], P(('grp', 'dev')), may hold values from -6 to 6
- edge_latent: bfloat16 [32, 384, 256], P(('grp', 'dev')), may hold values from -6 to 6
- cut_latent: bfloat16 [32, 5, 64, 256], P(('grp', 'dev')), may hold values from -6 to 6
- node_cotangent: bfloat16 [32, 128, 256], P(('grp', 'dev')), may hold values from -6 to 6
- edge_sender: int32 [32, 384], P(('grp', 'dev')), may hold values from 0 to 127, as said below
- edge_receiver: int32 [32, 384], P(('grp', 'dev')), may hold values from 0 to 127, as said below
- boundary_rows: int32 [32, 5, 16], P(('grp', 'dev')), may hold values from 0 to 127, as said below
- cut_slot: int32 [32, 5, 64], P(('grp', 'dev')), may hold values from 0 to 15
- cut_receiver: int32 [32, 5, 64], P(('grp', 'dev')), may hold values from 0 to 127, as said below
- node_count: int32 [32], P(('grp', 'dev')), may hold values from 64 to 128, as said below
- edge_count: int32 [32], P(('grp', 'dev')), may hold values from 192 to 384, as said below
- edge_first: bfloat16 [768, 256], replicated, may hold values from -0.21875 to 0.21875
- edge_second: bfloat16 [256, 256], replicated, may hold values from -0.375 to 0.375
- edge_gain: float32 [256], replicated, may hold values from 0.1 to 1.9
- node_first: bfloat16 [512, 256], replicated, may hold values from -0.25 to 0.25
- node_second: bfloat16 [256, 256], replicated, may hold values from -0.375 to 0.375
- node_gain: float32 [256], replicated, may hold values from 0.1 to 1.9
Outputs:
- updated_nodes: bfloat16 [32, 128, 256], P(('grp', 'dev'))
- node_gradient: bfloat16 [32, 128, 256], P(('grp', 'dev'))
- edge_gradient: bfloat16 [32, 384, 256], P(('grp', 'dev'))
- cut_gradient: bfloat16 [32, 5, 64, 256], P(('grp', 'dev'))
The draws below stay inside these ranges and needn't reach their ends.
Inputs may be any that keep to these rules, and one draw needn't show every extreme that they name: Nodes at or beyond a partition's node_count are padding. Inner edges at or beyond a partition's edge_count are padding. `edge_sender`: a node of the partition below its node_count. `edge_receiver`: a node of the partition below its node_count. `boundary_rows`: a node of the partition below its node_count; a node may stand more than once. `cut_receiver`: a node of the partition below its node_count.
All inputs are finite; a program needn't handle non-finite values.
Results may differ from the reference program's by a relative error of at most 0.0095.
Values may be sent and summed in bfloat16 or wider, within the bound.
No kernel may reach another device: no remote copies, remote signals or barrier semaphores. Data moves between devices by JAX's collectives and lax.ppermute only.
A program may use at most 64 MiB of HBM per device.

```python
import jax
import jax.numpy as jnp
from jax import lax

L = 256
NODE_DEV = 128
ROUNDS = 5
EDGE_DEV = 384
SEND = 16
CUT = 64
PARTS_SIZE = 32
N_DEV = 8


def count_table(key, limit, salt):
    counts = jax.random.randint(jax.random.fold_in(key, salt), (PARTS_SIZE,), limit // 2, limit + 1)
    fullest = jax.random.randint(jax.random.fold_in(key, salt + 1), (), 0, PARTS_SIZE)
    counts = jnp.where(jnp.arange(PARTS_SIZE) == fullest, limit, counts)
    return (counts.astype(jnp.int32), fullest)


def local_indices(key, salt, shape):
    counts, fullest = count_table(key, NODE_DEV, 11)
    raw = jax.random.randint(jax.random.fold_in(key, salt), shape, 0, 1 << 20)
    spread = counts.reshape((PARTS_SIZE,) + (1,) * (len(shape) - 1))
    values = raw % spread
    corner = (fullest,) + (0,) * (len(shape) - 1)
    values = values.at[corner].set(NODE_DEV - 1)
    return values.astype(jnp.int32)


def draw_node_count(key, part):
    counts, fullest = count_table(key, NODE_DEV, 11)
    return counts


def draw_edge_count(key, part):
    counts, fullest = count_table(key, EDGE_DEV, 31)
    return counts


def draw_edge_sender(key, part):
    return local_indices(key, 21, (PARTS_SIZE, EDGE_DEV))


def draw_edge_receiver(key, part):
    return local_indices(key, 22, (PARTS_SIZE, EDGE_DEV))


def draw_boundary_rows(key, part):
    return local_indices(key, 23, (PARTS_SIZE, ROUNDS, SEND))


def draw_cut_receiver(key, part):
    return local_indices(key, 24, (PARTS_SIZE, ROUNDS, CUT))


def with_ends(result, own_key, smallest, top_value):
    index_at = [jax.random.randint(jax.random.fold_in(own_key, axis), (), 0, length) for axis, length in enumerate(result.shape)]
    widest = result.shape.index(max(result.shape))
    beside = index_at[:widest] + [(index_at[widest] + 1) % result.shape[widest]] + index_at[widest + 1:]
    return result.at[tuple(index_at)].set(smallest).at[tuple(beside)].set(top_value)


def block_levels(key, shape, cuts, least, high):
    factor_of, own = 1.0, jax.random.fold_in(key, 6)
    for axis_at, blocks in cuts:
        heights = jnp.exp(jax.random.uniform(jax.random.fold_in(own, axis_at), (blocks,), jnp.float32, least / len(cuts), high / len(cuts)))
        factor_of = factor_of * jnp.repeat(heights, shape[axis_at] // blocks).reshape([-1 if axis == axis_at else 1 for axis in range(len(shape))])
    return factor_of


def scatter_about(stream_key, dims, width, bound, split=(), kind=jnp.bfloat16):
    drawn = width * jax.random.normal(stream_key, dims, jnp.float32)
    if split:
        drawn = drawn * block_levels(stream_key, dims, split, -0.22, 0.18)
    return jnp.clip(drawn, -bound, bound).astype(kind)


def setup_inputs(seed: int = 0) -> dict:
    splits = jax.random.split(jax.random.key(seed), 18)
    return {
        "node_latent": scatter_about(splits[0], (PARTS_SIZE, NODE_DEV, L), 1.0, 6.0, ((0, 32),)),
        "edge_latent": scatter_about(splits[1], (PARTS_SIZE, EDGE_DEV, L), 1.0, 6.0, ((0, 32),)),
        "cut_latent": scatter_about(splits[2], (PARTS_SIZE, ROUNDS, CUT, L), 1.0, 6.0, ((0, 32),)),
        "node_cotangent": scatter_about(splits[3], (PARTS_SIZE, NODE_DEV, L), 1.0, 6.0, ((0, 32),)),
        "edge_sender": draw_edge_sender(jax.random.fold_in(splits[17], 71), 0),
        "edge_receiver": draw_edge_receiver(jax.random.fold_in(splits[17], 71), 0),
        "boundary_rows": draw_boundary_rows(jax.random.fold_in(splits[17], 71), 0),
        "cut_slot": with_ends(jax.random.randint(splits[7], (PARTS_SIZE, ROUNDS, CUT), 0, SEND), jax.random.fold_in(splits[7], 1), 0, SEND - 1).astype(jnp.int32),
        "cut_receiver": draw_cut_receiver(jax.random.fold_in(splits[17], 71), 0),
        "node_count": draw_node_count(jax.random.fold_in(splits[17], 71), 0),
        "edge_count": draw_edge_count(jax.random.fold_in(splits[17], 71), 0),
        "edge_first": scatter_about(splits[11], (3 * L, L), (3 * L) ** -0.5, 0.21875),
        "edge_second": scatter_about(splits[12], (L, L), L ** -0.5, 0.375),
        "edge_gain": jnp.clip(1.0 + 0.18 * jax.random.normal(splits[13], (L,), jnp.float32), 0.1, 1.9),
        "node_first": scatter_about(splits[14], (2 * L, L), (2 * L) ** -0.5, 0.25),
        "node_second": scatter_about(splits[15], (L, L), L ** -0.5, 0.375),
        "node_gain": jnp.clip(1.0 + 0.18 * jax.random.normal(splits[16], (L,), jnp.float32), 0.1, 1.9),
    }


epsilon = 1e-05

def layer_norm(values, gain):
    centre = lax.optimization_barrier(jnp.mean(values, axis=-1, keepdims=True))
    centred = values - centre
    variance = lax.optimization_barrier(jnp.mean(centred * centred, axis=-1, keepdims=True))
    inverse = 1.0 / jnp.sqrt(variance + epsilon)
    normed = centred * inverse
    return (normed * gain, normed, inverse)

def norm_backward(upstream, gain, normed, inverse):
    scaled = upstream * gain
    first_mean = lax.optimization_barrier(jnp.mean(scaled, axis=-1, keepdims=True))
    second_mean = lax.optimization_barrier(jnp.mean(scaled * normed, axis=-1, keepdims=True))
    return inverse * (scaled - first_mean - normed * second_mean)

def silu_slope(values):
    sigmoid = jax.nn.sigmoid(values)
    return sigmoid * (1.0 + values * (1.0 - sigmoid))

def partner_of(parts, round_index):
    if round_index < 2:
        return jnp.bitwise_xor(parts, N_DEV * 2 ** round_index)
    return jnp.bitwise_xor(parts, 2 ** (round_index - 2))

def pick_rows(table, indices):
    return table[indices]

def local_pass(inputs, weights):
    nodes, edges, cut_edges, cotangent, senders, receivers_local, slots, cut_targets, count_nodes, count_edges, incoming = inputs
    edge_first, edge_second, edge_gain, node_first, node_second, node_gain = weights
    valid = (jnp.arange(NODE_DEV) < count_nodes).astype(jnp.float32)[:, None]
    used = (jnp.arange(EDGE_DEV) < count_edges).astype(jnp.float32)
    cut_flat = cut_targets.reshape(-1)
    sender_rows = jax.vmap(pick_rows)(incoming, slots).reshape(-1, L)
    local_input = jnp.concatenate([nodes[receivers_local], nodes[senders], edges], 1)
    cut_input = jnp.concatenate([nodes[cut_flat], sender_rows, cut_edges.reshape(-1, L)], 1)
    edge_input = jnp.concatenate([local_input, cut_input], 0)
    receivers = jnp.concatenate([receivers_local, cut_flat])
    mask = jnp.concatenate([used, jnp.ones((cut_flat.shape[0],), jnp.float32)])[:, None]
    pre_edge = jnp.dot(edge_input, edge_first, preferred_element_type=jnp.float32)
    act_edge = jax.nn.silu(pre_edge).astype(jnp.bfloat16)
    out_edge = jnp.dot(act_edge, edge_second, preferred_element_type=jnp.float32)
    normed_edge, edge_normed, edge_inverse = layer_norm(out_edge, edge_gain)
    message = normed_edge * mask
    received_sum = jnp.zeros((NODE_DEV, L), jnp.float32).at[receivers].add(message)
    node_input = jnp.concatenate([nodes, received_sum.astype(jnp.bfloat16)], 1)
    pre_node = jnp.dot(node_input, node_first, preferred_element_type=jnp.float32)
    act_node = jax.nn.silu(pre_node).astype(jnp.bfloat16)
    out_node = jnp.dot(act_node, node_second, preferred_element_type=jnp.float32)
    normed_node, node_normed, node_inverse = layer_norm(out_node, node_gain)
    updated = ((nodes.astype(jnp.float32) + normed_node) * valid).astype(jnp.bfloat16)
    masked_cotangent = cotangent.astype(jnp.float32) * valid
    grad_out_node = norm_backward(masked_cotangent, node_gain, node_normed, node_inverse).astype(jnp.bfloat16)
    grad_act_node = jnp.dot(grad_out_node, node_second.T, preferred_element_type=jnp.float32)
    grad_pre_node = (grad_act_node * silu_slope(pre_node)).astype(jnp.bfloat16)
    grad_node_input = jnp.dot(grad_pre_node, node_first.T, preferred_element_type=jnp.float32)
    grad_message = grad_node_input[:, L:][receivers] * mask
    grad_out_edge = norm_backward(grad_message, edge_gain, edge_normed, edge_inverse).astype(jnp.bfloat16)
    grad_act_edge = jnp.dot(grad_out_edge, edge_second.T, preferred_element_type=jnp.float32)
    grad_pre_edge = (grad_act_edge * silu_slope(pre_edge)).astype(jnp.bfloat16)
    grad_edge_input = jnp.dot(grad_pre_edge, edge_first.T, preferred_element_type=jnp.float32)
    gradient = masked_cotangent + grad_node_input[:, :L]
    gradient = gradient.at[receivers].add(grad_edge_input[:, :L])
    gradient = gradient.at[senders].add(grad_edge_input[:EDGE_DEV, L:2 * L])
    edge_gradient = grad_edge_input[:EDGE_DEV, 2 * L:].astype(jnp.bfloat16)
    cut_gradient = grad_edge_input[EDGE_DEV:, 2 * L:].reshape(ROUNDS, CUT, L).astype(jnp.bfloat16)
    sender_part = grad_edge_input[EDGE_DEV:, L:2 * L].reshape(ROUNDS, CUT, L)

    def slot_sum(slot_ids, values):
        return jnp.zeros((SEND, L), jnp.float32).at[slot_ids].add(values)
    slot_sums = jax.vmap(slot_sum)(slots, sender_part)
    return (updated, gradient, edge_gradient, cut_gradient, slot_sums)

def add_rows(gradient, rows, values):
    return gradient.at[rows].add(values)

def reference(node_latent, edge_latent, cut_latent, node_cotangent, edge_sender, edge_receiver, boundary_rows, cut_slot, cut_receiver, node_count, edge_count, edge_first, edge_second, edge_gain, node_first, node_second, node_gain):
    parts = jnp.arange(PARTS_SIZE, dtype=jnp.int32)
    partners = [partner_of(parts, round_index) for round_index in range(ROUNDS)]
    sent = jax.vmap(pick_rows)(node_latent, boundary_rows)
    incoming = jnp.stack([sent[partners[round_index], round_index] for round_index in range(ROUNDS)], 1)
    weights = (edge_first, edge_second, edge_gain, node_first, node_second, node_gain)

    def one_part(inputs):
        return local_pass(inputs, weights)
    updated, gradient, edge_gradient, cut_gradient, slot_sums = lax.map(one_part, (node_latent, edge_latent, cut_latent, node_cotangent, edge_sender, edge_receiver, cut_slot, cut_receiver, node_count, edge_count, incoming))
    for round_index in range(ROUNDS):
        returned = slot_sums[partners[round_index], round_index]
        gradient = jax.vmap(add_rows)(gradient, boundary_rows[:, round_index], returned)
    return (updated, gradient.astype(jnp.bfloat16), edge_gradient, cut_gradient)
```

```python
import functools

import jax
import jax.numpy as jnp
from jax import lax
from jax.experimental import pallas as pl
from jax.experimental.pallas import tpu as pltpu
from jax.sharding import PartitionSpec as P

ROUNDS = 5
GRP_ROUNDS = 2

epsilon = 1e-05

bf16 = jnp.bfloat16
f32 = jnp.float32


def partner(shard, round_index):
    axis, apart = ("grp", round_index) if round_index < GRP_ROUNDS else ("dev", round_index - GRP_ROUNDS)
    return lax.ppermute(shard, axis, [(i, i ^ 1 << apart) for i in range(lax.axis_size(axis))])


def mm(a, b):
    return jnp.dot(a, b, preferred_element_type=f32)


def mm_t(a, b):
    return lax.dot_general(a, b, (((1,), (1,)), ((), ())), preferred_element_type=f32)


def t_mm(a, b):
    return lax.dot_general(a, b, (((0,), (0,)), ((), ())), preferred_element_type=f32)


def hot(row, count):
    shape = (count, row.shape[1])
    return (lax.broadcasted_iota(jnp.int32, shape, 0) == jnp.broadcast_to(row, shape)).astype(f32)


def lane_mean(values):
    return jnp.mean(values, axis=-1, keepdims=True)


def norm_parts(values):
    centred = values - lane_mean(values)
    inverse = lax.rsqrt(lane_mean(centred * centred) + epsilon)
    return centred * inverse, inverse


def norm_backward(scaled, normed, inverse):
    return inverse * (scaled - lane_mean(scaled) - normed * lane_mean(scaled * normed))


def silu_parts(values):
    sigmoid = jax.nn.sigmoid(values)
    act = values * sigmoid
    return act, sigmoid + act * (1.0 - sigmoid)


def send_kernel(nodes, boundary, *out):
    table = jnp.concatenate([hot(boundary[r], nodes.shape[0]) for r in range(ROUNDS)], 1)
    rows = t_mm(table.astype(bf16), nodes[...]).astype(bf16)
    send = boundary.shape[2]
    for r in range(ROUNDS):
        out[r][...] = rows[r * send : (r + 1) * send]


def main_kernel(
    node_count, edge_count, nodes, edges, cuts, cotangent, sender, receiver, slot, cut_receiver,
    edge_first, edge_second, edge_gain, node_first, node_second, node_gain,
    *rest,
):
    arrived = rest[:ROUNDS]
    updated, base, grad_pre = rest[ROUNDS : ROUNDS + 3]
    back = rest[ROUNDS + 3 :]
    n, width = nodes.shape
    e = edges.shape[0]
    send = arrived[0].shape[0]
    x = nodes[...]
    edge_lane = lax.broadcasted_iota(jnp.int32, (1, e), 1)
    receive_inner = jnp.where(edge_lane < edge_count[0], receiver[...], -1)
    hot_receive = jnp.concatenate(
        [hot(receive_inner, n)] + [hot(cut_receiver[r], n) for r in range(ROUNDS)], 1
    )
    slots = jnp.concatenate([slot[r] + r * send for r in range(ROUNDS)], 1)
    hot_slot = hot(slots, 128)
    hot_send = hot(sender[...], n)
    gather_receive = hot_receive.T.astype(bf16)
    gather_send = jnp.concatenate([hot_send, hot_slot], 1).T.astype(bf16)
    scatter_receive = hot_receive.astype(bf16)

    w1 = edge_first[:width]
    w2 = edge_first[width : 2 * width]
    w3 = edge_first[2 * width :]
    far = jnp.concatenate([a[...] for a in arrived] + [jnp.zeros((128 - ROUNDS * send, width), bf16)], 0)
    by_receiver = mm(x, w1).astype(bf16)
    by_sender = mm(jnp.concatenate([x, far], 0), w2).astype(bf16)
    gather_inner = jnp.concatenate([gather_receive[:e], gather_send[:e]], 1)
    gather_cut = jnp.concatenate([gather_receive[e:], gather_send[e:]], 1)
    pre_inner = mm(gather_inner, jnp.concatenate([by_receiver, by_sender[:n]], 0)) + mm(edges[...], w3)
    pre_cut = mm(gather_cut, jnp.concatenate([by_receiver, by_sender[n:]], 0)) + mm(cuts[...], w3)
    pre = jnp.concatenate([pre_inner, pre_cut], 0)
    act, slope = silu_parts(pre)
    normed, inverse = norm_parts(mm(act.astype(bf16), edge_second[...]))
    received = mm(scatter_receive, normed.astype(bf16)) * edge_gain[...]

    valid = lax.broadcasted_iota(jnp.int32, (n, 1), 0) < node_count[0]
    pre_node = mm(jnp.concatenate([x, received.astype(bf16)], 1), node_first[...])
    act_node, slope_node = silu_parts(pre_node)
    normed_node, inverse_node = norm_parts(mm(act_node.astype(bf16), node_second[...]))
    updated[...] = jnp.where(valid, x.astype(f32) + normed_node * node_gain[...], 0.0).astype(bf16)
    masked = jnp.where(valid, cotangent[...].astype(f32), 0.0)
    grad_out_node = norm_backward(masked * node_gain[...], normed_node, inverse_node).astype(bf16)
    grad_pre_node = (mm_t(grad_out_node, node_second[...]) * slope_node).astype(bf16)
    base[...] = masked + mm_t(grad_pre_node, node_first[:width])
    at_receiver = mm_t(grad_pre_node, node_first[width:]) * edge_gain[...]
    high = at_receiver.astype(bf16)
    low = (at_receiver - high.astype(f32)).astype(bf16)
    scaled = mm(jnp.concatenate([gather_receive, gather_receive], 1), jnp.concatenate([high, low], 0))
    grad_out = norm_backward(scaled, normed, inverse).astype(bf16)
    grad = (mm_t(grad_out, edge_second[...]) * slope).astype(bf16)
    grad_pre[...] = grad
    sums = mm(hot_slot.astype(bf16), grad[e:]).astype(bf16)
    for r in range(ROUNDS):
        back[r][...] = sums[r * send : (r + 1) * send]


def last_kernel(
    base, grad_pre, sender, receiver, cut_receiver, boundary, edge_first, *rest
):
    arrived = rest[:ROUNDS]
    node_gradient, edge_gradient, cut_gradient = rest[ROUNDS:]
    n, width = base.shape
    e = edge_gradient.shape[0]
    grad = grad_pre[...]
    by_edge = mm_t(grad, edge_first[2 * width :]).astype(bf16)
    edge_gradient[...] = by_edge[:e]
    cut_gradient[...] = by_edge[e:]
    hot_receive = jnp.concatenate(
        [hot(receiver[...], n)] + [hot(cut_receiver[r], n) for r in range(ROUNDS)], 1
    ).astype(bf16)
    hot_boundary = jnp.concatenate([hot(boundary[r], n) for r in range(ROUNDS)], 1).astype(bf16)
    at_receiver = mm(hot_receive, grad).astype(bf16)
    far = jnp.concatenate([a[...] for a in arrived], 0)
    at_sender = (mm(hot(sender[...], n).astype(bf16), grad[:e]) + mm(hot_boundary, far)).astype(bf16)
    total = base[...] + mm_t(at_receiver, edge_first[:width]) + mm_t(at_sender, edge_first[width : 2 * width])
    node_gradient[...] = total.astype(bf16)


VMEM = pl.BlockSpec(memory_space=pltpu.VMEM)
SMEM = pl.BlockSpec(memory_space=pltpu.SMEM)


def call(kernel, out_shape, in_specs, args, flops):
    size = sum(a.size * a.dtype.itemsize for a in list(args) + list(out_shape))
    return pl.pallas_call(
        kernel,
        out_shape=out_shape,
        in_specs=in_specs,
        out_specs=[VMEM] * len(out_shape),
        compiler_params=pltpu.CompilerParams(vmem_limit_bytes=32 * 1024 * 1024),
        cost_estimate=pl.CostEstimate(flops=flops, bytes_accessed=size, transcendentals=0),
    )(*args)


def shards(
    node_latent, edge_latent, cut_latent, node_cotangent, edge_sender, edge_receiver, boundary_rows,
    cut_slot, cut_receiver, node_count, edge_count, edge_first, edge_second, edge_gain, node_first,
    node_second, node_gain,
):
    nodes = node_latent[0]
    edges = edge_latent[0]
    cuts = cut_latent[0].reshape(-1, cut_latent.shape[-1])
    n, width = nodes.shape
    e, c = edges.shape[0], cuts.shape[0]
    boundary = boundary_rows.transpose(1, 0, 2)
    slot = cut_slot.transpose(1, 0, 2)
    cut_targets = cut_receiver.transpose(1, 0, 2)
    send = boundary.shape[2]
    shape = jax.ShapeDtypeStruct
    sent = call(
        send_kernel, [shape((send, width), bf16)] * ROUNDS, [VMEM] * 2, (nodes, boundary),
        2 * 128 * n * width,
    )
    arrived = [partner(sent[r], r) for r in range(ROUNDS)]
    outs = call(
        main_kernel,
        [shape((n, width), bf16), shape((n, width), f32), shape((e + c, width), bf16)]
        + [shape((send, width), bf16)] * ROUNDS,
        [SMEM] * 2 + [VMEM] * (14 + ROUNDS),
        (
            node_count, edge_count, nodes, edges, cuts, node_cotangent[0], edge_sender, edge_receiver, slot,
            cut_targets, edge_first, edge_second, edge_gain[None], node_first, node_second, node_gain[None],
            *arrived,
        ),
        2 * (e + c) * width * width * 6,
    )
    updated, base, grad_pre = outs[:3]
    returned = [partner(outs[3 + r], r) for r in range(ROUNDS)]
    node_gradient, edge_gradient, cut_gradient = call(
        last_kernel,
        [shape((n, width), bf16), shape((e, width), bf16), shape((c, width), bf16)],
        [VMEM] * (7 + ROUNDS),
        (base, grad_pre, edge_sender, edge_receiver, cut_targets, boundary, edge_first, *returned),
        2 * (e + c) * width * width * 2,
    )
    return (
        updated[None],
        node_gradient[None],
        edge_gradient[None],
        cut_gradient.reshape(cut_latent.shape),
    )


def solution(mesh):
    part = ("grp", "dev")
    placed = tuple(P(part, *[None] * (d - 1)) for d in (3, 3, 4, 3, 2, 2, 3, 3, 3, 1, 1)) + (P(),) * 6
    return jax.shard_map(
        shards,
        mesh=mesh,
        in_specs=placed,
        out_specs=tuple(P(part, *[None] * (d - 1)) for d in (3, 3, 3, 4)),
        check_vma=False,
    )
```

```python
import functools

import jax
import jax.numpy as jnp
from jax import lax
from jax.experimental import pallas as pl
from jax.experimental.pallas import tpu as pltpu
from jax.sharding import PartitionSpec as P

ROUNDS = 5
GRP_ROUNDS = 2

epsilon = 1e-05

bf16 = jnp.bfloat16
f32 = jnp.float32


def partner(shard, round_index):
    axis, apart = ("grp", round_index) if round_index < GRP_ROUNDS else ("dev", round_index - GRP_ROUNDS)
    return lax.ppermute(shard, axis, [(i, i ^ 1 << apart) for i in range(lax.axis_size(axis))])


def exchange(rows):
    got = lax.optimization_barrier([partner(rows[r], r) for r in reversed(range(ROUNDS))])
    return got[::-1]


def mm(a, b):
    return jnp.dot(a, b, preferred_element_type=f32)


def mm_t(a, b):
    return lax.dot_general(a, b, (((1,), (1,)), ((), ())), preferred_element_type=f32)


def t_mm(a, b):
    return lax.dot_general(a, b, (((0,), (0,)), ((), ())), preferred_element_type=f32)


def hot(row, count):
    shape = (count, row.shape[1])
    return (lax.broadcasted_iota(jnp.int32, shape, 0) == jnp.broadcast_to(row, shape)).astype(f32)


def lane_mean(values):
    return jnp.mean(values, axis=-1, keepdims=True)


def norm_parts(values):
    centred = values - lane_mean(values)
    inverse = lax.rsqrt(lane_mean(centred * centred) + epsilon)
    return centred * inverse, inverse


def norm_backward(scaled, normed, inverse):
    return inverse * (scaled - lane_mean(scaled) - normed * lane_mean(scaled * normed))


def silu_parts(values):
    sigmoid = jax.nn.sigmoid(values)
    act = values * sigmoid
    return act, sigmoid + act * (1.0 - sigmoid)


def load(held, loaded, done):
    copies = [pltpu.make_async_copy(h, v, done.at[i]) for i, (h, v) in enumerate(zip(held, loaded))]
    for copy in copies:
        copy.start()
    return copies


def send_kernel(count, *rest):
    held, loaded, out, done = rest[:count], rest[count : 2 * count], rest[2 * count : -1], rest[-1]
    copies = load(held, loaded, done)
    for copy in copies[:2]:
        copy.wait()
    nodes, boundary = loaded[:2]
    table = jnp.concatenate([hot(boundary[r], nodes.shape[0]) for r in range(ROUNDS)], 1)
    rows = t_mm(table.astype(bf16), nodes[...]).astype(bf16)
    send = boundary.shape[2]
    for r in range(ROUNDS):
        out[r][...] = rows[r * send : (r + 1) * send]
    for copy in copies[2:]:
        copy.wait()


def inner_kernel(*rest):
    counts, nodes, edges, sender, receiver, edge_first, edge_second = rest[:7]
    by_receiver, gather_out, normed_out, inverse_out, slope_out, received = rest[7:]
    n, width = nodes.shape
    e = edges.shape[0]
    used = lax.broadcasted_iota(jnp.int32, (1, e), 1) < counts[1:, :e]
    hot_receive = hot(jnp.where(used, receiver[...], -1), n)
    gather = jnp.concatenate([hot_receive, hot(sender[...], n)], 0).T.astype(bf16)
    first = mm(nodes[...], edge_first[:width]).astype(bf16)
    second = mm(nodes[...], edge_first[width : 2 * width]).astype(bf16)
    pre = mm(gather, jnp.concatenate([first, second], 0)) + mm(edges[...], edge_first[2 * width :])
    act, slope = silu_parts(pre)
    normed, inverse = norm_parts(mm(act.astype(bf16), edge_second[...]))
    by_receiver[...] = first
    gather_out[...] = gather[:, :n]
    normed_out[...] = normed
    inverse_out[...] = inverse
    slope_out[...] = slope
    received[...] = mm(hot_receive.astype(bf16), normed.astype(bf16))


def main_kernel(
    counts, nodes, cuts, cotangent, slot, cut_receiver, edge_first, edge_second, edge_gain, node_first, node_second,
    node_gain, by_receiver, received_inner, *rest,
):
    arrived = rest[:ROUNDS]
    updated, base, gained, grad_cut = rest[ROUNDS : ROUNDS + 4]
    back = rest[ROUNDS + 4 :]
    n, width = nodes.shape
    send = arrived[0].shape[0]
    x = nodes[...]
    hot_receive = jnp.concatenate([hot(cut_receiver[r], n) for r in range(ROUNDS)], 1)
    hot_slot = hot(jnp.concatenate([slot[r] + r * send for r in range(ROUNDS)], 1), 128)
    gather = jnp.concatenate([hot_receive, hot_slot], 0).T.astype(bf16)
    far = jnp.concatenate([a[...] for a in arrived] + [jnp.zeros((128 - ROUNDS * send, width), bf16)], 0)
    by_sender = mm(far, edge_first[width : 2 * width]).astype(bf16)
    pre = mm(gather, jnp.concatenate([by_receiver[...], by_sender], 0)) + mm(cuts[...], edge_first[2 * width :])
    act, slope = silu_parts(pre)
    normed, inverse = norm_parts(mm(act.astype(bf16), edge_second[...]))
    received = (received_inner[...] + mm(hot_receive.astype(bf16), normed.astype(bf16))) * edge_gain[...]

    valid = lax.broadcasted_iota(jnp.int32, (n, width), 0) < counts[:1, :width]
    pre_node = mm(jnp.concatenate([x, received.astype(bf16)], 1), node_first[...])
    act_node, slope_node = silu_parts(pre_node)
    normed_node, inverse_node = norm_parts(mm(act_node.astype(bf16), node_second[...]))
    updated[...] = jnp.where(valid, x.astype(f32) + normed_node * node_gain[...], 0.0).astype(bf16)
    masked = jnp.where(valid, cotangent[...].astype(f32), 0.0)
    grad_out_node = norm_backward(masked * node_gain[...], normed_node, inverse_node).astype(bf16)
    grad_pre_node = (mm_t(grad_out_node, node_second[...]) * slope_node).astype(bf16)
    at_receiver = mm_t(grad_pre_node, node_first[width:]) * edge_gain[...]
    high = at_receiver.astype(bf16)
    low = (at_receiver - high.astype(f32)).astype(bf16)
    parts = jnp.concatenate([high, low], 0)
    twice = jnp.concatenate([gather[:, :n], gather[:, :n]], 1)
    grad_out = norm_backward(mm(twice, parts), normed, inverse).astype(bf16)
    grad = (mm_t(grad_out, edge_second[...]) * slope).astype(bf16)
    sums = mm(hot_slot.astype(bf16), grad).astype(bf16)
    for r in range(ROUNDS):
        back[r][...] = sums[r * send : (r + 1) * send]
    grad_cut[...] = grad
    gained[...] = parts
    base[...] = masked + mm_t(grad_pre_node, node_first[:width])


def outer_kernel(
    gained, gather, normed, inverse, slope, edge_first, edge_second, sender, receiver, cut_receiver, grad_cut, base,
    updated_in, updated, edge_gradient, cut_gradient, total,
):
    n, width = base.shape
    updated[...] = updated_in[...]
    cut = grad_cut[...]
    cut_gradient[...] = mm_t(cut, edge_first[2 * width :]).astype(bf16)
    twice = jnp.concatenate([gather[...], gather[...]], 1)
    grad_out = norm_backward(mm(twice, gained[...]), normed[...], inverse[...]).astype(bf16)
    grad = (mm_t(grad_out, edge_second[...]) * slope[...]).astype(bf16)
    edge_gradient[...] = mm_t(grad, edge_first[2 * width :]).astype(bf16)
    hot_cut = jnp.concatenate([hot(cut_receiver[r], n) for r in range(ROUNDS)], 1).astype(bf16)
    at_receiver = mm(hot(receiver[...], n).astype(bf16), grad) + mm(hot_cut, cut)
    at_sender = mm(hot(sender[...], n).astype(bf16), grad)
    total[...] = (
        base[...]
        + mm_t(at_receiver.astype(bf16), edge_first[:width])
        + mm_t(at_sender.astype(bf16), edge_first[width : 2 * width])
    )


def last_kernel(total, boundary, edge_first, *rest):
    arrived, node_gradient = rest[:ROUNDS], rest[ROUNDS]
    n, width = total.shape
    table = jnp.concatenate([hot(boundary[r], n) for r in range(ROUNDS)], 1).astype(bf16)
    at_sender = mm(table, jnp.concatenate([a[...] for a in arrived], 0)).astype(bf16)
    node_gradient[...] = (total[...] + mm_t(at_sender, edge_first[width : 2 * width])).astype(bf16)


VMEM = pl.BlockSpec(memory_space=pltpu.VMEM)
HBM = pl.BlockSpec(memory_space=pltpu.HBM)


def call(kernel, out_shape, args, flops, held=(), scratch=()):
    size = sum(a.size * a.dtype.itemsize for a in args + tuple(held))
    return pl.pallas_call(
        kernel,
        out_shape=out_shape,
        in_specs=[VMEM] * len(args) + [HBM] * len(held),
        out_specs=[VMEM] * len(out_shape),
        scratch_shapes=scratch,
        compiler_params=pltpu.CompilerParams(vmem_limit_bytes=32 * 1024 * 1024),
        cost_estimate=pl.CostEstimate(flops=flops, bytes_accessed=size, transcendentals=0),
    )(*args, *(pltpu.with_memory_space_constraint(a, pltpu.HBM) for a in held))


def shards(
    node_latent, edge_latent, cut_latent, node_cotangent, edge_sender, edge_receiver, boundary_rows,
    cut_slot, cut_receiver, node_count, edge_count, edge_first, edge_second, edge_gain, node_first,
    node_second, node_gain,
):
    nodes = node_latent[0]
    edges = edge_latent[0]
    cuts = cut_latent[0].reshape(-1, cut_latent.shape[-1])
    n, width = nodes.shape
    e, c = edges.shape[0], cuts.shape[0]
    boundary = boundary_rows.transpose(1, 0, 2)
    slot = cut_slot.transpose(1, 0, 2)
    cut_targets = cut_receiver.transpose(1, 0, 2)
    send = boundary.shape[2]
    shape = jax.ShapeDtypeStruct
    kept = pltpu.VMEM

    def copies(arrays):
        return [kept(a.shape, a.dtype) for a in arrays]

    held = (
        nodes, boundary, edge_receiver, edge_sender, edge_first, edges, edge_second, slot,
        cut_targets, edge_gain[None], node_gain[None],
    )
    outs = call(
        functools.partial(send_kernel, len(held)),
        copies(held) + [kept((send, width), bf16)] * ROUNDS,
        (),
        2 * 128 * n * width,
        held,
        [pltpu.SemaphoreType.DMA((len(held),))],
    )
    (
        nodes, boundary, edge_receiver, edge_sender, edge_first, edges, edge_second, slot,
        cut_targets, edge_gain, node_gain,
    ) = outs[: len(held)]
    sent = outs[len(held) :]
    counts = lax.broadcast_in_dim(jnp.concatenate([node_count, edge_count]), (2, max(e, width)), (0,))
    arrived = exchange(sent)
    outs = call(
        inner_kernel,
        [
            kept((n, width), bf16), kept((e, n), bf16), kept((e, width), f32), kept((e, 1), f32),
            kept((e, width), f32), kept((n, width), f32),
        ],
        (counts, nodes, edges, edge_sender, edge_receiver, edge_first, edge_second),
        2 * e * width * width * 4,
    )
    by_receiver, gather, normed, inverse, slope, received = outs
    outs = call(
        main_kernel,
        [kept((n, width), bf16), kept((n, width), f32), kept((2 * n, width), bf16), kept((c, width), bf16)]
        + [kept((send, width), bf16)] * ROUNDS,
        (
            counts, nodes, cuts, node_cotangent[0], slot, cut_targets, edge_first, edge_second, edge_gain, node_first,
            node_second, node_gain, by_receiver, received, *arrived,
        ),
        2 * c * width * width * 6,
    )
    updated, base, gained, grad_cut = outs[:4]
    returned = exchange(outs[4:])
    updated, edge_gradient, cut_gradient, total = call(
        outer_kernel,
        [shape((n, width), bf16), shape((e, width), bf16), shape((c, width), bf16), kept((n, width), f32)],
        (
            gained, gather, normed, inverse, slope, edge_first, edge_second, edge_sender, edge_receiver,
            cut_targets, grad_cut, base, updated,
        ),
        2 * (e + c) * width * width * 3,
    )
    (node_gradient,) = call(
        last_kernel,
        [shape((n, width), bf16)],
        (total, boundary, edge_first, *returned),
        2 * 2 * n * width * width,
    )
    return (
        updated[None],
        node_gradient[None],
        edge_gradient[None],
        cut_gradient.reshape(cut_latent.shape),
    )


def solution(mesh):
    part = ("grp", "dev")
    placed = tuple(P(part, *[None] * (d - 1)) for d in (3, 3, 4, 3, 2, 2, 3, 3, 3, 1, 1)) + (P(),) * 6
    return jax.shard_map(
        shards,
        mesh=mesh,
        in_specs=placed,
        out_specs=tuple(P(part, *[None] * (d - 1)) for d in (3, 3, 3, 4)),
        check_vma=False,
    )
```

```python
import functools

import jax
import jax.numpy as jnp
from jax import lax
from jax.experimental import pallas as pl
from jax.experimental.pallas import tpu as pltpu
from jax.sharding import PartitionSpec as P

ROUNDS = 5
LONG = 4 * 10**9
GRP_ROUNDS = 2

epsilon = 1e-05

bf16 = jnp.bfloat16
f32 = jnp.float32


def partner(shard, round_index):
    axis, apart = ("grp", round_index) if round_index < GRP_ROUNDS else ("dev", round_index - GRP_ROUNDS)
    return lax.ppermute(shard, axis, [(i, i ^ 1 << apart) for i in range(lax.axis_size(axis))])


def exchange(rows):
    got = lax.optimization_barrier([partner(rows[r], r) for r in reversed(range(ROUNDS))])
    return got[::-1]


def mm(a, b):
    return jnp.dot(a, b, preferred_element_type=f32)


def mm_t(a, b):
    return lax.dot_general(a, b, (((1,), (1,)), ((), ())), preferred_element_type=f32)


def t_mm(a, b):
    return lax.dot_general(a, b, (((0,), (0,)), ((), ())), preferred_element_type=f32)


def hot(row, count):
    shape = (count, row.shape[1])
    return (lax.broadcasted_iota(jnp.int32, shape, 0) == jnp.broadcast_to(row, shape)).astype(f32)


def lane_mean(values):
    return jnp.mean(values, axis=-1, keepdims=True)


def norm_parts(values):
    centred = values - lane_mean(values)
    inverse = lax.rsqrt(lane_mean(centred * centred) + epsilon)
    return centred * inverse, inverse


def norm_backward(scaled, normed, inverse):
    return inverse * (scaled - lane_mean(scaled) - normed * lane_mean(scaled * normed))


def silu_parts(values):
    sigmoid = jax.nn.sigmoid(values)
    act = values * sigmoid
    return act, sigmoid + act * (1.0 - sigmoid)


def load(held, loaded, done):
    copies = [pltpu.make_async_copy(h, v, done.at[i]) for i, (h, v) in enumerate(zip(held, loaded))]
    for copy in copies:
        copy.start()
    return copies


def send_kernel(count, *rest):
    held, loaded, out, done = rest[:count], rest[count : 2 * count], rest[2 * count : -1], rest[-1]
    copies = load(held, loaded, done)
    boundary, nodes = loaded[:2]
    copies[0].wait()
    table = jnp.concatenate([hot(boundary[r], nodes.shape[0]) for r in range(ROUNDS)], 1).T.astype(bf16)
    copies[1].wait()
    rows = mm(table, nodes[...]).astype(bf16)
    send = boundary.shape[2]
    for r in range(ROUNDS):
        out[r][...] = rows[r * send : (r + 1) * send]
    for copy in copies[2:]:
        copy.wait()


def inner_kernel(*rest):
    edge_count, nodes, edges, sender, receiver, edge_first, edge_second = rest[:7]
    by_receiver, gather_out, normed_out, inverse_out, slope_out, received = rest[7:]
    n, width = nodes.shape
    e = edges.shape[0]
    used = lax.broadcasted_iota(jnp.int32, (1, e), 1) < edge_count[0]
    hot_receive = hot(jnp.where(used, receiver[...], -1), n)
    gather = jnp.concatenate([hot_receive, hot(sender[...], n)], 0).T.astype(bf16)
    first = mm(nodes[...], edge_first[:width]).astype(bf16)
    second = mm(nodes[...], edge_first[width : 2 * width]).astype(bf16)
    pre = mm(gather, jnp.concatenate([first, second], 0)) + mm(edges[...], edge_first[2 * width :])
    act, slope = silu_parts(pre)
    normed, inverse = norm_parts(mm(act.astype(bf16), edge_second[...]))
    by_receiver[...] = first
    gather_out[...] = gather[:, :n]
    normed_out[...] = normed
    inverse_out[...] = inverse
    slope_out[...] = slope
    received[...] = mm(hot_receive.astype(bf16), normed.astype(bf16))


def main_kernel(
    node_count, nodes, cuts, cotangent, slot, cut_receiver, edge_first, edge_second, edge_gain, node_first, node_second,
    node_gain, by_receiver, received_inner, *rest,
):
    arrived = rest[:ROUNDS]
    updated, base, gained, grad_cut = rest[ROUNDS : ROUNDS + 4]
    back = rest[ROUNDS + 4 :]
    n, width = nodes.shape
    send = arrived[0].shape[0]
    x = nodes[...]
    hot_receive = jnp.concatenate([hot(cut_receiver[r], n) for r in range(ROUNDS)], 1)
    hot_slot = hot(jnp.concatenate([slot[r] + r * send for r in range(ROUNDS)], 1), 128)
    gather = jnp.concatenate([hot_receive, hot_slot], 0).T.astype(bf16)
    far = jnp.concatenate([a[...] for a in arrived] + [jnp.zeros((128 - ROUNDS * send, width), bf16)], 0)
    by_sender = mm(far, edge_first[width : 2 * width]).astype(bf16)
    pre = mm(gather, jnp.concatenate([by_receiver[...], by_sender], 0)) + mm(cuts[...], edge_first[2 * width :])
    act, slope = silu_parts(pre)
    normed, inverse = norm_parts(mm(act.astype(bf16), edge_second[...]))
    received = (received_inner[...] + mm(hot_receive.astype(bf16), normed.astype(bf16))) * edge_gain[...]

    valid = lax.broadcasted_iota(jnp.int32, (n, width), 0) < node_count[0]
    pre_node = mm(jnp.concatenate([x, received.astype(bf16)], 1), node_first[...])
    act_node, slope_node = silu_parts(pre_node)
    normed_node, inverse_node = norm_parts(mm(act_node.astype(bf16), node_second[...]))
    updated[...] = jnp.where(valid, x.astype(f32) + normed_node * node_gain[...], 0.0).astype(bf16)
    masked = jnp.where(valid, cotangent[...].astype(f32), 0.0)
    grad_out_node = norm_backward(masked * node_gain[...], normed_node, inverse_node).astype(bf16)
    grad_pre_node = (mm_t(grad_out_node, node_second[...]) * slope_node).astype(bf16)
    at_receiver = mm_t(grad_pre_node, node_first[width:]) * edge_gain[...]
    high = at_receiver.astype(bf16)
    low = (at_receiver - high.astype(f32)).astype(bf16)
    parts = jnp.concatenate([high, low], 0)
    twice = jnp.concatenate([gather[:, :n], gather[:, :n]], 1)
    grad_out = norm_backward(mm(twice, parts), normed, inverse).astype(bf16)
    grad = (mm_t(grad_out, edge_second[...]) * slope).astype(bf16)
    sums = mm(hot_slot[:96].astype(bf16), grad).astype(bf16)
    for r in range(ROUNDS):
        back[r][...] = sums[r * send : (r + 1) * send]
    grad_cut[...] = grad
    gained[...] = parts
    base[...] = masked + mm_t(grad_pre_node, node_first[:width])


def outer_kernel(
    gained, gather, normed, inverse, slope, edge_first, edge_second, sender, receiver, cut_receiver, grad_cut, base,
    updated_in, boundary, updated, edge_gradient, cut_gradient, total, table, second,
):
    n, width = base.shape
    updated[...] = updated_in[...]
    table[...] = jnp.concatenate([hot(boundary[r], n) for r in range(ROUNDS)], 1).astype(bf16)
    second[...] = edge_first[width : 2 * width].T
    cut = grad_cut[...]
    cut_gradient[...] = mm_t(cut, edge_first[2 * width :]).astype(bf16)
    twice = jnp.concatenate([gather[...], gather[...]], 1)
    grad_out = norm_backward(mm(twice, gained[...]), normed[...], inverse[...]).astype(bf16)
    grad = (mm_t(grad_out, edge_second[...]) * slope[...]).astype(bf16)
    edge_gradient[...] = mm_t(grad, edge_first[2 * width :]).astype(bf16)
    hot_cut = jnp.concatenate([hot(cut_receiver[r], n) for r in range(ROUNDS)], 1).astype(bf16)
    at_receiver = mm(hot(receiver[...], n).astype(bf16), grad) + mm(hot_cut, cut)
    at_sender = mm(hot(sender[...], n).astype(bf16), grad)
    total[...] = (
        base[...]
        + mm_t(at_receiver.astype(bf16), edge_first[:width])
        + mm_t(at_sender.astype(bf16), edge_first[width : 2 * width])
    )


def last_kernel(total, table, second, *rest):
    arrived, node_gradient = rest[:ROUNDS], rest[ROUNDS]
    at_sender = mm(table[...], jnp.concatenate([a[...] for a in arrived], 0)).astype(bf16)
    node_gradient[...] = (total[...] + mm(at_sender, second[...])).astype(bf16)


VMEM = pl.BlockSpec(memory_space=pltpu.VMEM)
HBM = pl.BlockSpec(memory_space=pltpu.HBM)
SMEM = pl.BlockSpec(memory_space=pltpu.SMEM)


def call(kernel, out_shape, args, flops, held=(), scratch=()):
    size = sum(a.size * a.dtype.itemsize for a in args + tuple(held))
    return pl.pallas_call(
        kernel,
        out_shape=out_shape,
        in_specs=[SMEM if a.ndim == 1 else VMEM for a in args] + [HBM] * len(held),
        out_specs=[VMEM] * len(out_shape),
        scratch_shapes=scratch,
        compiler_params=pltpu.CompilerParams(vmem_limit_bytes=32 * 1024 * 1024),
        cost_estimate=pl.CostEstimate(flops=flops, bytes_accessed=size, transcendentals=0),
    )(*args, *(pltpu.with_memory_space_constraint(a, pltpu.HBM) for a in held))


def shards(
    node_latent, edge_latent, cut_latent, node_cotangent, edge_sender, edge_receiver, boundary_rows,
    cut_slot, cut_receiver, node_count, edge_count, edge_first, edge_second, edge_gain, node_first,
    node_second, node_gain,
):
    nodes = node_latent[0]
    edges = edge_latent[0]
    cuts = cut_latent[0].reshape(-1, cut_latent.shape[-1])
    n, width = nodes.shape
    e, c = edges.shape[0], cuts.shape[0]
    boundary = boundary_rows.transpose(1, 0, 2)
    slot = cut_slot.transpose(1, 0, 2)
    cut_targets = cut_receiver.transpose(1, 0, 2)
    send = boundary.shape[2]
    shape = jax.ShapeDtypeStruct
    kept = pltpu.VMEM

    def copies(arrays):
        return [kept(a.shape, a.dtype) for a in arrays]

    held = (boundary, nodes, edge_receiver, edge_sender, slot, cut_targets, edge_gain[None], node_gain[None])
    outs = call(
        functools.partial(send_kernel, len(held)),
        copies(held) + [kept((send, width), bf16)] * ROUNDS,
        (),
        LONG,
        held,
        [pltpu.SemaphoreType.DMA((len(held),))],
    )
    boundary, nodes, edge_receiver, edge_sender, slot, cut_targets, edge_gain, node_gain = outs[: len(held)]
    sent = outs[len(held) :]
    arrived = exchange(sent)
    outs = call(
        inner_kernel,
        [
            kept((n, width), bf16), kept((e, n), bf16), kept((e, width), f32), kept((e, 1), f32),
            kept((e, width), f32), kept((n, width), f32),
        ],
        (edge_count, nodes, edges, edge_sender, edge_receiver, edge_first, edge_second),
        LONG,
    )
    by_receiver, gather, normed, inverse, slope, received = outs
    outs = call(
        main_kernel,
        [kept((n, width), bf16), kept((n, width), f32), kept((2 * n, width), bf16), kept((c, width), bf16)]
        + [kept((send, width), bf16)] * ROUNDS,
        (
            node_count, nodes, cuts, node_cotangent[0], slot, cut_targets, edge_first, edge_second, edge_gain, node_first,
            node_second, node_gain, by_receiver, received, *arrived,
        ),
        2 * c * width * width * 6,
    )
    updated, base, gained, grad_cut = outs[:4]
    returned = exchange(outs[4:])
    updated, edge_gradient, cut_gradient, total, table, second = call(
        outer_kernel,
        [
            shape((n, width), bf16), shape((e, width), bf16), shape((c, width), bf16), kept((n, width), f32),
            kept((n, ROUNDS * send), bf16), kept((width, width), bf16),
        ],
        (
            gained, gather, normed, inverse, slope, edge_first, edge_second, edge_sender, edge_receiver,
            cut_targets, grad_cut, base, updated, boundary,
        ),
        2 * (e + c) * width * width * 3,
    )
    (node_gradient,) = call(
        last_kernel,
        [shape((n, width), bf16)],
        (total, table, second, *returned),
        2 * 2 * n * width * width,
    )
    return (
        updated[None],
        node_gradient[None],
        edge_gradient[None],
        cut_gradient.reshape(cut_latent.shape),
    )


def solution(mesh):
    part = ("grp", "dev")
    placed = tuple(P(part, *[None] * (d - 1)) for d in (3, 3, 4, 3, 2, 2, 3, 3, 3, 1, 1)) + (P(),) * 6
    return jax.shard_map(
        shards,
        mesh=mesh,
        in_specs=placed,
        out_specs=tuple(P(part, *[None] * (d - 1)) for d in (3, 3, 3, 4)),
        check_vma=False,
    )
```

```python
import functools

import jax
import jax.numpy as jnp
from jax import lax
from jax.experimental import pallas as pl
from jax.experimental.pallas import tpu as pltpu
from jax.sharding import PartitionSpec as P

ROUNDS = 5
GRP_ROUNDS = 2
LONG = 4 * 10**9

epsilon = 1e-05

bf16 = jnp.bfloat16
f32 = jnp.float32


def partner(shard, round_index):
    axis, apart = ("grp", round_index) if round_index < GRP_ROUNDS else ("dev", round_index - GRP_ROUNDS)
    return lax.ppermute(shard, axis, [(i, i ^ 1 << apart) for i in range(lax.axis_size(axis))])


def exchange(rows):
    got = lax.optimization_barrier([partner(rows[r], r) for r in reversed(range(ROUNDS))])
    return got[::-1]


def mm(a, b):
    return jnp.dot(a, b, preferred_element_type=f32)


def mm_t(a, b):
    return lax.dot_general(a, b, (((1,), (1,)), ((), ())), preferred_element_type=f32)


def hot(row, count):
    shape = (count, row.shape[1])
    return (lax.broadcasted_iota(jnp.int32, shape, 0) == jnp.broadcast_to(row, shape)).astype(f32)


def split(values):
    high = values.astype(bf16)
    return high, (values - high.astype(f32)).astype(bf16)


def add_rows(table, values):
    return mm(jnp.concatenate([table, table], 1), jnp.concatenate(split(values), 0))


def lane_mean(values):
    return jnp.mean(values, axis=-1, keepdims=True)


def norm_parts(values):
    centred = values - lane_mean(values)
    inverse = lax.rsqrt(lane_mean(centred * centred) + epsilon)
    return centred * inverse, inverse


def norm_backward(scaled, normed, inverse):
    return inverse * (scaled - lane_mean(scaled) - normed * lane_mean(scaled * normed))


def silu_parts(values):
    sigmoid = jax.nn.sigmoid(values)
    act = values * sigmoid
    return act, sigmoid + act * (1.0 - sigmoid)


def load(held, loaded, done):
    copies = [pltpu.make_async_copy(h, v, done.at[i]) for i, (h, v) in enumerate(zip(held, loaded))]
    for copy in copies:
        copy.start()
    return copies


def send_kernel(count, *rest):
    held, loaded, out, done = rest[:count], rest[count : 2 * count], rest[2 * count : -1], rest[-1]
    copies = load(held, loaded, done)
    boundary, nodes = loaded[:2]
    copies[0].wait()
    table = jnp.concatenate([hot(boundary[r], nodes.shape[0]) for r in range(ROUNDS)], 1).T.astype(bf16)
    copies[1].wait()
    rows = mm(table, nodes[...]).astype(bf16)
    send = boundary.shape[2]
    for r in range(ROUNDS):
        out[r][...] = rows[r * send : (r + 1) * send]
    for copy in copies[2:]:
        copy.wait()


def inner_kernel(*rest):
    edge_count, nodes, edges, sender, receiver, edge_first, edge_second = rest[:7]
    by_receiver, gather_out, normed_out, inverse_out, slope_out, received = rest[7:]
    n, width = nodes.shape
    e = edges.shape[0]
    used = lax.broadcasted_iota(jnp.int32, (1, e), 1) < edge_count[0]
    hot_receive = hot(jnp.where(used, receiver[...], -1), n)
    gather = jnp.concatenate([hot_receive, hot(sender[...], n)], 0).T.astype(bf16)
    first = mm(nodes[...], edge_first[:width])
    second = mm(nodes[...], edge_first[width : 2 * width])
    pre = add_rows(gather, jnp.concatenate([first, second], 0)) + mm(edges[...], edge_first[2 * width :])
    act, slope = silu_parts(pre)
    normed, inverse = norm_parts(mm(act.astype(bf16), edge_second[...]))
    by_receiver[...] = jnp.concatenate(split(first), 0)
    gather_out[...] = gather[:, :n]
    normed_out[...] = normed
    inverse_out[...] = inverse
    slope_out[...] = slope
    received[...] = add_rows(hot_receive.astype(bf16), normed)


def main_kernel(
    node_count, nodes, cuts, cotangent, slot, cut_receiver, edge_first, edge_second, edge_gain, node_first, node_second,
    node_gain, by_receiver, received_inner, *rest,
):
    arrived = rest[:ROUNDS]
    updated, base, gained, grad_cut = rest[ROUNDS : ROUNDS + 4]
    back = rest[ROUNDS + 4 :]
    n, width = nodes.shape
    send = arrived[0].shape[0]
    x = nodes[...]
    hot_receive = jnp.concatenate([hot(cut_receiver[r], n) for r in range(ROUNDS)], 1)
    hot_slot = hot(jnp.concatenate([slot[r] + r * send for r in range(ROUNDS)], 1), 128)
    gather = hot_receive.T.astype(bf16)
    twice = jnp.concatenate([gather, gather], 1)
    near = mm(twice, by_receiver[...]) + mm(cuts[...], edge_first[2 * width :])
    far = jnp.concatenate([a[...] for a in arrived] + [jnp.zeros((128 - ROUNDS * send, width), bf16)], 0)
    pre = near + add_rows(hot_slot.T.astype(bf16), mm(far, edge_first[width : 2 * width]))
    act, slope = silu_parts(pre)
    normed, inverse = norm_parts(mm(act.astype(bf16), edge_second[...]))
    received = (received_inner[...] + add_rows(hot_receive.astype(bf16), normed)) * edge_gain[...]

    valid = lax.broadcasted_iota(jnp.int32, (n, width), 0) < node_count[0]
    pre_node = mm(jnp.concatenate([x, received.astype(bf16)], 1), node_first[...])
    act_node, slope_node = silu_parts(pre_node)
    normed_node, inverse_node = norm_parts(mm(act_node.astype(bf16), node_second[...]))
    updated[...] = jnp.where(valid, x.astype(f32) + normed_node * node_gain[...], 0.0).astype(bf16)
    masked = jnp.where(valid, cotangent[...].astype(f32), 0.0)
    grad_out_node = norm_backward(masked * node_gain[...], normed_node, inverse_node).astype(bf16)
    grad_pre_node = (mm_t(grad_out_node, node_second[...]) * slope_node).astype(bf16)
    at_receiver = mm_t(grad_pre_node, node_first[width:]) * edge_gain[...]
    parts = jnp.concatenate(split(at_receiver), 0)
    grad_out = norm_backward(mm(twice, parts), normed, inverse).astype(bf16)
    grad = (mm_t(grad_out, edge_second[...]) * slope).astype(bf16)
    sums = mm(hot_slot[:96].astype(bf16), grad).astype(bf16)
    for r in range(ROUNDS):
        back[r][...] = sums[r * send : (r + 1) * send]
    grad_cut[...] = grad
    gained[...] = parts
    base[...] = masked + mm_t(grad_pre_node, node_first[:width])


def outer_kernel(
    gained, gather, normed, inverse, slope, edge_first, edge_second, sender, receiver, cut_receiver, grad_cut, base,
    updated_in, boundary, updated, edge_gradient, cut_gradient, total, table, second,
):
    n, width = base.shape
    updated[...] = updated_in[...]
    table[...] = jnp.concatenate([hot(boundary[r], n) for r in range(ROUNDS)], 1).astype(bf16)
    second[...] = edge_first[width : 2 * width].T
    cut = grad_cut[...]
    cut_gradient[...] = mm_t(cut, edge_first[2 * width :]).astype(bf16)
    twice = jnp.concatenate([gather[...], gather[...]], 1)
    grad_out = norm_backward(mm(twice, gained[...]), normed[...], inverse[...]).astype(bf16)
    grad = (mm_t(grad_out, edge_second[...]) * slope[...]).astype(bf16)
    edge_gradient[...] = mm_t(grad, edge_first[2 * width :]).astype(bf16)
    hot_cut = jnp.concatenate([hot(cut_receiver[r], n) for r in range(ROUNDS)], 1).astype(bf16)
    at_receiver = mm(hot(receiver[...], n).astype(bf16), grad) + mm(hot_cut, cut)
    at_sender = mm(hot(sender[...], n).astype(bf16), grad)
    total[...] = (
        base[...]
        + mm_t(at_receiver.astype(bf16), edge_first[:width])
        + mm_t(at_sender.astype(bf16), edge_first[width : 2 * width])
    )


def last_kernel(total, table, second, *rest):
    arrived, node_gradient = rest[:ROUNDS], rest[ROUNDS]
    at_sender = mm(table[...], jnp.concatenate([a[...] for a in arrived], 0)).astype(bf16)
    node_gradient[...] = (total[...] + mm(at_sender, second[...])).astype(bf16)


VMEM = pl.BlockSpec(memory_space=pltpu.VMEM)
HBM = pl.BlockSpec(memory_space=pltpu.HBM)
SMEM = pl.BlockSpec(memory_space=pltpu.SMEM)


def call(kernel, out_shape, args, flops, held=(), scratch=()):
    size = sum(a.size * a.dtype.itemsize for a in args + tuple(held))
    return pl.pallas_call(
        kernel,
        out_shape=out_shape,
        in_specs=[SMEM if a.ndim == 1 else VMEM for a in args] + [HBM] * len(held),
        out_specs=[VMEM] * len(out_shape),
        scratch_shapes=scratch,
        compiler_params=pltpu.CompilerParams(vmem_limit_bytes=32 * 1024 * 1024),
        cost_estimate=pl.CostEstimate(flops=flops, bytes_accessed=size, transcendentals=0),
    )(*args, *(pltpu.with_memory_space_constraint(a, pltpu.HBM) for a in held))


def shards(
    node_latent, edge_latent, cut_latent, node_cotangent, edge_sender, edge_receiver, boundary_rows,
    cut_slot, cut_receiver, node_count, edge_count, edge_first, edge_second, edge_gain, node_first,
    node_second, node_gain,
):
    nodes = node_latent[0]
    edges = edge_latent[0]
    cuts = cut_latent[0].reshape(-1, cut_latent.shape[-1])
    n, width = nodes.shape
    e, c = edges.shape[0], cuts.shape[0]
    boundary = boundary_rows.transpose(1, 0, 2)
    slot = cut_slot.transpose(1, 0, 2)
    cut_targets = cut_receiver.transpose(1, 0, 2)
    send = boundary.shape[2]
    shape = jax.ShapeDtypeStruct
    kept = pltpu.VMEM

    def copies(arrays):
        return [kept(a.shape, a.dtype) for a in arrays]

    held = (boundary, nodes, edge_receiver, edge_sender, slot, cut_targets, edge_gain[None], node_gain[None])
    outs = call(
        functools.partial(send_kernel, len(held)),
        copies(held) + [kept((send, width), bf16)] * ROUNDS,
        (),
        LONG,
        held,
        [pltpu.SemaphoreType.DMA((len(held),))],
    )
    boundary, nodes, edge_receiver, edge_sender, slot, cut_targets, edge_gain, node_gain = outs[: len(held)]
    sent = outs[len(held) :]
    arrived = exchange(sent)
    outs = call(
        inner_kernel,
        [
            kept((2 * n, width), bf16), kept((e, n), bf16), kept((e, width), f32), kept((e, 1), f32),
            kept((e, width), f32), kept((n, width), f32),
        ],
        (edge_count, nodes, edges, edge_sender, edge_receiver, edge_first, edge_second),
        LONG,
    )
    by_receiver, gather, normed, inverse, slope, received = outs
    outs = call(
        main_kernel,
        [kept((n, width), bf16), kept((n, width), f32), kept((2 * n, width), bf16), kept((c, width), bf16)]
        + [kept((send, width), bf16)] * ROUNDS,
        (
            node_count, nodes, cuts, node_cotangent[0], slot, cut_targets, edge_first, edge_second, edge_gain, node_first,
            node_second, node_gain, by_receiver, received, *arrived,
        ),
        2 * c * width * width * 6,
    )
    updated, base, gained, grad_cut = outs[:4]
    returned = exchange(outs[4:])
    updated, edge_gradient, cut_gradient, total, table, second = call(
        outer_kernel,
        [
            shape((n, width), bf16), shape((e, width), bf16), shape((c, width), bf16), kept((n, width), f32),
            kept((n, ROUNDS * send), bf16), kept((width, width), bf16),
        ],
        (
            gained, gather, normed, inverse, slope, edge_first, edge_second, edge_sender, edge_receiver,
            cut_targets, grad_cut, base, updated, boundary,
        ),
        2 * (e + c) * width * width * 3,
    )
    (node_gradient,) = call(
        last_kernel,
        [shape((n, width), bf16)],
        (total, table, second, *returned),
        2 * 2 * n * width * width,
    )
    return (
        updated[None],
        node_gradient[None],
        edge_gradient[None],
        cut_gradient.reshape(cut_latent.shape),
    )


def solution(mesh):
    part = ("grp", "dev")
    placed = tuple(P(part, *[None] * (d - 1)) for d in (3, 3, 4, 3, 2, 2, 3, 3, 3, 1, 1)) + (P(),) * 6
    return jax.shard_map(
        shards,
        mesh=mesh,
        in_specs=placed,
        out_specs=tuple(P(part, *[None] * (d - 1)) for d in (3, 3, 3, 4)),
        check_vma=False,
    )
```

```python
import functools

import jax
import jax.numpy as jnp
from jax import lax
from jax.experimental import pallas as pl
from jax.experimental.pallas import tpu as pltpu
from jax.sharding import PartitionSpec as P

ROUNDS = 5
GRP_ROUNDS = 2
LONG = 4 * 10**9

epsilon = 1e-05

bf16 = jnp.bfloat16
f32 = jnp.float32


def partner(shard, round_index):
    axis, apart = ("grp", round_index) if round_index < GRP_ROUNDS else ("dev", round_index - GRP_ROUNDS)
    return lax.ppermute(shard, axis, [(i, i ^ 1 << apart) for i in range(lax.axis_size(axis))])


def exchange(rows):
    got = lax.optimization_barrier([partner(rows[r], r) for r in reversed(range(ROUNDS))])
    return got[::-1]


def mm(a, b):
    return jnp.dot(a, b, preferred_element_type=f32)


def mm_t(a, b):
    return lax.dot_general(a, b, (((1,), (1,)), ((), ())), preferred_element_type=f32)


def hot(row, count):
    shape = (count, row.shape[1])
    return (lax.broadcasted_iota(jnp.int32, shape, 0) == jnp.broadcast_to(row, shape)).astype(f32)


def split(values):
    high = values.astype(bf16)
    return high, (values - high.astype(f32)).astype(bf16)


def add_rows(table, values):
    return mm(jnp.concatenate([table, table], 1), jnp.concatenate(split(values), 0))


def lane_mean(values):
    return jnp.mean(values, axis=-1, keepdims=True)


def norm_parts(values):
    centred = values - lane_mean(values)
    inverse = lax.rsqrt(lane_mean(centred * centred) + epsilon)
    return centred * inverse, inverse


def norm_backward(scaled, normed, inverse):
    return inverse * (scaled - lane_mean(scaled) - normed * lane_mean(scaled * normed))


def silu_parts(values):
    sigmoid = jax.nn.sigmoid(values)
    act = values * sigmoid
    return act, sigmoid + act * (1.0 - sigmoid)


def load(held, loaded, done):
    copies = [pltpu.make_async_copy(h, v, done.at[i]) for i, (h, v) in enumerate(zip(held, loaded))]
    for copy in copies:
        copy.start()
    return copies


def send_kernel(count, *rest):
    held, loaded, out, done = rest[:count], rest[count : 2 * count], rest[2 * count : -1], rest[-1]
    copies = load(held, loaded, done)
    boundary, nodes = loaded[:2]
    copies[0].wait()
    table = jnp.concatenate([hot(boundary[r], nodes.shape[0]) for r in range(ROUNDS)], 1).T.astype(bf16)
    copies[1].wait()
    rows = mm(table, nodes[...]).astype(bf16)
    send = boundary.shape[2]
    for r in range(ROUNDS):
        out[r][...] = rows[r * send : (r + 1) * send]
    for copy in copies[2:]:
        copy.wait()


def inner_kernel(
    edge_count, nodes, edges, cuts, sender, receiver, slot, cut_receiver, boundary, edge_first, edge_second,
    gather_out, normed_out, inverse_out, slope_out, received, near, gather_cut, gather_far,
    scatter_receive, scatter_send, scatter_cut, scatter_far, scatter_boundary, first_t, second_t,
):
    n, width = nodes.shape
    e = edges.shape[0]
    used = lax.broadcasted_iota(jnp.int32, (1, e), 1) < edge_count[0]
    hot_receive = hot(jnp.where(used, receiver[...], -1), n)
    hot_send = hot(sender[...], n)
    gather = jnp.concatenate([hot_receive, hot_send], 0).T.astype(bf16)
    first = mm(nodes[...], edge_first[:width])
    second = mm(nodes[...], edge_first[width : 2 * width])
    pre = add_rows(gather, jnp.concatenate([first, second], 0)) + mm(edges[...], edge_first[2 * width :])
    act, slope = silu_parts(pre)
    normed, inverse = norm_parts(mm(act.astype(bf16), edge_second[...]))
    gather_out[...] = gather[:, :n]
    normed_out[...] = normed
    inverse_out[...] = inverse
    slope_out[...] = slope
    received[...] = add_rows(hot_receive.astype(bf16), normed)
    scatter_receive[...] = hot_receive.astype(bf16)
    scatter_send[...] = hot_send.astype(bf16)

    send = boundary.shape[2]
    hot_cut = jnp.concatenate([hot(cut_receiver[r], n) for r in range(ROUNDS)], 1)
    hot_far = hot(jnp.concatenate([slot[r] + r * send for r in range(ROUNDS)], 1), gather_far.shape[1])
    at_cut = hot_cut.T.astype(bf16)
    near[...] = add_rows(at_cut, first) + mm(cuts[...], edge_first[2 * width :])
    gather_cut[...] = at_cut
    gather_far[...] = hot_far.T.astype(bf16)
    scatter_cut[...] = hot_cut.astype(bf16)
    scatter_far[...] = hot_far[: scatter_far.shape[0]].astype(bf16)
    scatter_boundary[...] = jnp.concatenate([hot(boundary[r], n) for r in range(ROUNDS)], 1).astype(bf16)
    first_t[...] = edge_first[...].T
    second_t[...] = edge_second[...].T


def main_kernel(
    nodes, cotangent, edge_first, edge_second, edge_gain, node_first, node_second, node_gain, received_inner, near,
    gather_cut, gather_far, scatter_cut, scatter_far, second_t, *rest,
):
    arrived = rest[:ROUNDS]
    updated, base, gained, grad_cut = rest[ROUNDS : ROUNDS + 4]
    back = rest[ROUNDS + 4 :]
    n, width = nodes.shape
    send = arrived[0].shape[0]
    x = nodes[...]
    empty = jnp.zeros((gather_far.shape[1] - ROUNDS * send, width), bf16)
    far = jnp.concatenate([a[...] for a in arrived] + [empty], 0)
    pre = near[...] + add_rows(gather_far[...], mm(far, edge_first[width : 2 * width]))
    act, slope = silu_parts(pre)
    normed, inverse = norm_parts(mm(act.astype(bf16), edge_second[...]))
    received = (received_inner[...] + add_rows(scatter_cut[...], normed)) * edge_gain[...]

    pre_node = mm(jnp.concatenate([x, received.astype(bf16)], 1), node_first[...])
    act_node, slope_node = silu_parts(pre_node)
    normed_node, inverse_node = norm_parts(mm(act_node.astype(bf16), node_second[...]))
    updated[...] = (x.astype(f32) + normed_node * node_gain[...]).astype(bf16)
    upstream = cotangent[...].astype(f32)
    grad_out_node = norm_backward(upstream * node_gain[...], normed_node, inverse_node).astype(bf16)
    grad_pre_node = (mm_t(grad_out_node, node_second[...]) * slope_node).astype(bf16)
    at_receiver = mm_t(grad_pre_node, node_first[width:]) * edge_gain[...]
    parts = jnp.concatenate(split(at_receiver), 0)
    twice = jnp.concatenate([gather_cut[...], gather_cut[...]], 1)
    grad_out = norm_backward(mm(twice, parts), normed, inverse).astype(bf16)
    grad = (mm(grad_out, second_t[...]) * slope).astype(bf16)
    sums = mm(scatter_far[...], grad).astype(bf16)
    for r in range(ROUNDS):
        back[r][...] = sums[r * send : (r + 1) * send]
    grad_cut[...] = grad
    gained[...] = parts
    base[...] = upstream + mm_t(grad_pre_node, node_first[:width])


def outer_kernel(
    node_count, gained, gather, normed, inverse, slope, first_t, second_t, scatter_receive, scatter_send, scatter_cut,
    grad_cut, base, updated_in, updated, edge_gradient, cut_gradient, total,
):
    n, width = base.shape
    valid = lax.broadcasted_iota(jnp.int32, (n, width), 0) < node_count[0]
    updated[...] = jnp.where(valid, updated_in[...].astype(f32), 0.0).astype(bf16)
    cut = grad_cut[...]
    cut_gradient[...] = mm(cut, first_t[:, 2 * width :]).astype(bf16)
    twice = jnp.concatenate([gather[...], gather[...]], 1)
    grad_out = norm_backward(mm(twice, gained[...]), normed[...], inverse[...]).astype(bf16)
    grad = (mm(grad_out, second_t[...]) * slope[...]).astype(bf16)
    edge_gradient[...] = mm(grad, first_t[:, 2 * width :]).astype(bf16)
    at_receiver = mm(scatter_receive[...], grad) + mm(scatter_cut[...], cut)
    at_sender = mm(scatter_send[...], grad)
    total[...] = (
        jnp.where(valid, base[...], 0.0)
        + mm(at_receiver.astype(bf16), first_t[:, :width])
        + mm(at_sender.astype(bf16), first_t[:, width : 2 * width])
    )


def last_kernel(total, scatter_boundary, first_t, updated, edge_gradient, cut_gradient, *rest):
    arrived, outs, here, done = rest[:ROUNDS], rest[ROUNDS : ROUNDS + 4], *rest[ROUNDS + 4 :]
    held = (updated, edge_gradient, cut_gradient, here)
    copies = [pltpu.make_async_copy(a, b, done.at[i]) for i, (a, b) in enumerate(zip(held, outs))]
    for copy in copies[:3]:
        copy.start()
    width = total.shape[1]
    at_sender = mm(scatter_boundary[...], jnp.concatenate([a[...] for a in arrived], 0)).astype(bf16)
    here[...] = (total[...] + mm(at_sender, first_t[:, width : 2 * width])).astype(bf16)
    copies[3].start()
    for copy in copies:
        copy.wait()


VMEM = pl.BlockSpec(memory_space=pltpu.VMEM)
HBM = pl.BlockSpec(memory_space=pltpu.HBM)
SMEM = pl.BlockSpec(memory_space=pltpu.SMEM)


def call(kernel, out_shape, args, flops, held=(), scratch=(), written=0):
    size = sum(a.size * a.dtype.itemsize for a in args + tuple(held))
    return pl.pallas_call(
        kernel,
        out_shape=out_shape,
        in_specs=[SMEM if a.ndim == 1 else VMEM for a in args] + [HBM] * len(held),
        out_specs=[VMEM if i >= written else HBM for i in range(len(out_shape))],
        scratch_shapes=scratch,
        compiler_params=pltpu.CompilerParams(vmem_limit_bytes=32 * 1024 * 1024),
        cost_estimate=pl.CostEstimate(flops=flops, bytes_accessed=size if flops else 0, transcendentals=0),
    )(*args, *(pltpu.with_memory_space_constraint(a, pltpu.HBM) for a in held))


def shards(
    node_latent, edge_latent, cut_latent, node_cotangent, edge_sender, edge_receiver, boundary_rows,
    cut_slot, cut_receiver, node_count, edge_count, edge_first, edge_second, edge_gain, node_first,
    node_second, node_gain,
):
    nodes = node_latent[0]
    edges = edge_latent[0]
    cuts = cut_latent[0].reshape(-1, cut_latent.shape[-1])
    n, width = nodes.shape
    e, c = edges.shape[0], cuts.shape[0]
    boundary = boundary_rows.transpose(1, 0, 2)
    slot = cut_slot.transpose(1, 0, 2)
    cut_targets = cut_receiver.transpose(1, 0, 2)
    send = boundary.shape[2]
    shape = jax.ShapeDtypeStruct
    kept = pltpu.VMEM

    def copies(arrays):
        return [kept(a.shape, a.dtype) for a in arrays]

    held = (boundary, nodes, edge_receiver, edge_sender, slot, cut_targets, edge_gain[None], node_gain[None])
    outs = call(
        functools.partial(send_kernel, len(held)),
        copies(held) + [kept((send, width), bf16)] * ROUNDS,
        (),
        LONG,
        held,
        [pltpu.SemaphoreType.DMA((len(held),))],
    )
    boundary, nodes, edge_receiver, edge_sender, slot, cut_targets, edge_gain, node_gain = outs[: len(held)]
    sent = outs[len(held) :]
    arrived = exchange(sent)
    slots = ROUNDS * send
    some = -(-slots // 32) * 32
    all_slots = -(-slots // 128) * 128
    outs = call(
        inner_kernel,
        [
            kept((e, n), bf16), kept((e, width), f32), kept((e, 1), f32), kept((e, width), f32),
            kept((n, width), f32), kept((c, width), f32), kept((c, n), bf16), kept((c, all_slots), bf16),
            kept((n, e), bf16), kept((n, e), bf16), kept((n, c), bf16), kept((some, c), bf16),
            kept((n, slots), bf16), kept((width, 3 * width), bf16), kept((width, width), bf16),
        ],
        (
            edge_count, nodes, edges, cuts, edge_sender, edge_receiver, slot, cut_targets, boundary, edge_first,
            edge_second,
        ),
        LONG,
    )
    gather, normed, inverse, slope, received, near, gather_cut, gather_far = outs[:8]
    scatter_receive, scatter_send, scatter_cut, scatter_far, scatter_boundary, first_t, second_t = outs[8:]
    outs = call(
        main_kernel,
        [kept((n, width), bf16), kept((n, width), f32), kept((2 * n, width), bf16), kept((c, width), bf16)]
        + [kept((send, width), bf16)] * ROUNDS,
        (
            nodes, node_cotangent[0], edge_first, edge_second, edge_gain, node_first, node_second, node_gain,
            received, near, gather_cut, gather_far, scatter_cut, scatter_far, second_t, *arrived,
        ),
        2 * c * width * width * 6,
    )
    updated, base, gained, grad_cut = outs[:4]
    returned = exchange(outs[4:])
    updated, edge_gradient, cut_gradient, total = call(
        outer_kernel,
        [kept((n, width), bf16), kept((e, width), bf16), kept((c, width), bf16), kept((n, width), f32)],
        (
            node_count, gained, gather, normed, inverse, slope, first_t, second_t, scatter_receive, scatter_send,
            scatter_cut, grad_cut, base, updated,
        ),
        0,
    )
    updated, edge_gradient, cut_gradient, node_gradient = call(
        last_kernel,
        [shape((n, width), bf16), shape((e, width), bf16), shape((c, width), bf16), shape((n, width), bf16)],
        (total, scatter_boundary, first_t, updated, edge_gradient, cut_gradient, *returned),
        2 * 2 * n * width * width,
        scratch=[pltpu.VMEM((n, width), bf16), pltpu.SemaphoreType.DMA((4,))],
        written=4,
    )
    return (
        updated[None],
        node_gradient[None],
        edge_gradient[None],
        cut_gradient.reshape(cut_latent.shape),
    )


def solution(mesh):
    part = ("grp", "dev")
    placed = tuple(P(part, *[None] * (d - 1)) for d in (3, 3, 4, 3, 2, 2, 3, 3, 3, 1, 1)) + (P(),) * 6
    return jax.shard_map(
        shards,
        mesh=mesh,
        in_specs=placed,
        out_specs=tuple(P(part, *[None] * (d - 1)) for d in (3, 3, 3, 4)),
        check_vma=False,
    )
```

```python
import functools

import jax
import jax.numpy as jnp
from jax import lax
from jax.experimental import pallas as pl
from jax.experimental.pallas import tpu as pltpu
from jax.sharding import PartitionSpec as P

ROUNDS = 5
GRP_ROUNDS = 2
LONG = 4 * 10**9

epsilon = 1e-05

bf16 = jnp.bfloat16
f32 = jnp.float32


def partner(shard, round_index):
    axis, apart = ("grp", round_index) if round_index < GRP_ROUNDS else ("dev", round_index - GRP_ROUNDS)
    return lax.ppermute(shard, axis, [(i, i ^ 1 << apart) for i in range(lax.axis_size(axis))])


def exchange(rows):
    got = lax.optimization_barrier([partner(rows[r], r) for r in reversed(range(ROUNDS))])
    return got[::-1]


def mm(a, b):
    return jnp.dot(a, b, preferred_element_type=f32)


def mm_t(a, b):
    return lax.dot_general(a, b, (((1,), (1,)), ((), ())), preferred_element_type=f32)


def hot(row, count):
    shape = (count, row.shape[1])
    return (lax.broadcasted_iota(jnp.int32, shape, 0) == jnp.broadcast_to(row, shape)).astype(f32)


def split(values):
    high = values.astype(bf16)
    return high, (values - high.astype(f32)).astype(bf16)


def add_rows(table, values):
    return mm(jnp.concatenate([table, table], 1), jnp.concatenate(split(values), 0))


def lane_mean(values):
    return jnp.mean(values, axis=-1, keepdims=True)


def norm_parts(values):
    centred = values - lane_mean(values)
    inverse = lax.rsqrt(lane_mean(centred * centred) + epsilon)
    return centred * inverse, inverse


def norm_backward(scaled, normed, inverse):
    return inverse * (scaled - lane_mean(scaled) - normed * lane_mean(scaled * normed))


def silu_parts(values):
    sigmoid = jax.nn.sigmoid(values)
    act = values * sigmoid
    return act, sigmoid + act * (1.0 - sigmoid)


def load(held, loaded, done):
    copies = [pltpu.make_async_copy(h, v, done.at[i]) for i, (h, v) in enumerate(zip(held, loaded))]
    for copy in copies:
        copy.start()
    return copies


def send_kernel(count, *rest):
    held, loaded, out, done = rest[:count], rest[count : 2 * count], rest[2 * count : -1], rest[-1]
    copies = load(held, loaded, done)
    boundary, nodes = loaded[:2]
    copies[0].wait()
    table = jnp.concatenate([hot(boundary[r], nodes.shape[0]) for r in range(ROUNDS)], 1).T.astype(bf16)
    copies[1].wait()
    rows = mm(table, nodes[...]).astype(bf16)
    send = boundary.shape[2]
    for r in range(ROUNDS):
        out[r][...] = rows[r * send : (r + 1) * send]
    for copy in copies[2:]:
        copy.wait()


def inner_kernel(
    edge_count, nodes, edges, cuts, sender, receiver, slot, cut_receiver, boundary, edge_first, edge_second,
    gather_out, normed_out, inverse_out, slope_out, received, near, gather_cut, gather_far,
    scatter_receive, scatter_send, scatter_cut, scatter_far, scatter_boundary, first_t, second_t,
):
    n, width = nodes.shape
    e = edges.shape[0]
    used = lax.broadcasted_iota(jnp.int32, (1, e), 1) < edge_count[0]
    hot_receive = hot(jnp.where(used, receiver[...], -1), n)
    hot_send = hot(sender[...], n)
    hot_cut = jnp.concatenate([hot(cut_receiver[r], n) for r in range(ROUNDS)], 1)
    gather = jnp.concatenate([hot_receive, hot_send, hot_cut], 1).T.astype(bf16)
    ends = mm(gather, nodes[...]).astype(bf16)
    pre = mm(jnp.concatenate([ends[:e], ends[e : 2 * e], edges[...]], 1), edge_first[...])
    act, slope = silu_parts(pre)
    normed, inverse = norm_parts(mm(act.astype(bf16), edge_second[...]))
    gather_out[...] = gather[:e]
    normed_out[...] = normed
    inverse_out[...] = inverse
    slope_out[...] = slope
    received[...] = add_rows(hot_receive.astype(bf16), normed)
    scatter_receive[...] = hot_receive.astype(bf16)
    scatter_send[...] = hot_send.astype(bf16)

    send = boundary.shape[2]
    hot_far = hot(jnp.concatenate([slot[r] + r * send for r in range(ROUNDS)], 1), gather_far.shape[1])
    near[...] = mm(ends[2 * e :], edge_first[:width]) + mm(cuts[...], edge_first[2 * width :])
    gather_cut[...] = gather[2 * e :]
    gather_far[...] = hot_far.T.astype(bf16)
    scatter_cut[...] = hot_cut.astype(bf16)
    scatter_far[...] = hot_far[: scatter_far.shape[0]].astype(bf16)
    scatter_boundary[...] = jnp.concatenate([hot(boundary[r], n) for r in range(ROUNDS)], 1).astype(bf16)
    first_t[...] = edge_first[...].T
    second_t[...] = edge_second[...].T


def main_kernel(
    nodes, cotangent, edge_first, edge_second, edge_gain, node_first, node_second, node_gain, received_inner, near,
    gather_cut, gather_far, scatter_cut, scatter_far, second_t, *rest,
):
    arrived = rest[:ROUNDS]
    updated, base, gained, grad_cut = rest[ROUNDS : ROUNDS + 4]
    back = rest[ROUNDS + 4 :]
    n, width = nodes.shape
    send = arrived[0].shape[0]
    x = nodes[...]
    empty = jnp.zeros((gather_far.shape[1] - ROUNDS * send, width), bf16)
    far = jnp.concatenate([a[...] for a in arrived] + [empty], 0)
    far_end = mm(gather_far[...], far).astype(bf16)
    pre = near[...] + mm(far_end, edge_first[width : 2 * width])
    act, slope = silu_parts(pre)
    normed, inverse = norm_parts(mm(act.astype(bf16), edge_second[...]))
    received = (received_inner[...] + add_rows(scatter_cut[...], normed)) * edge_gain[...]

    pre_node = mm(jnp.concatenate([x, received.astype(bf16)], 1), node_first[...])
    act_node, slope_node = silu_parts(pre_node)
    normed_node, inverse_node = norm_parts(mm(act_node.astype(bf16), node_second[...]))
    updated[...] = (x.astype(f32) + normed_node * node_gain[...]).astype(bf16)
    upstream = cotangent[...].astype(f32)
    grad_out_node = norm_backward(upstream * node_gain[...], normed_node, inverse_node).astype(bf16)
    grad_pre_node = (mm_t(grad_out_node, node_second[...]) * slope_node).astype(bf16)
    at_receiver = mm_t(grad_pre_node, node_first[width:]) * edge_gain[...]
    parts = jnp.concatenate(split(at_receiver), 0)
    twice = jnp.concatenate([gather_cut[...], gather_cut[...]], 1)
    grad_out = norm_backward(mm(twice, parts), normed, inverse).astype(bf16)
    grad = (mm(grad_out, second_t[...]) * slope).astype(bf16)
    sums = mm(scatter_far[...], grad).astype(bf16)
    for r in range(ROUNDS):
        back[r][...] = sums[r * send : (r + 1) * send]
    grad_cut[...] = grad
    gained[...] = parts
    base[...] = upstream + mm_t(grad_pre_node, node_first[:width])


def outer_kernel(
    node_count, gained, gather, normed, inverse, slope, first_t, second_t, scatter_receive, scatter_send, scatter_cut,
    grad_cut, base, updated_in, updated, edge_gradient, cut_gradient, total,
):
    n, width = base.shape
    valid = lax.broadcasted_iota(jnp.int32, (n, width), 0) < node_count[0]
    updated[...] = jnp.where(valid, updated_in[...].astype(f32), 0.0).astype(bf16)
    cut = grad_cut[...]
    cut_gradient[...] = mm(cut, first_t[:, 2 * width :]).astype(bf16)
    twice = jnp.concatenate([gather[...], gather[...]], 1)
    grad_out = norm_backward(mm(twice, gained[...]), normed[...], inverse[...]).astype(bf16)
    grad = (mm(grad_out, second_t[...]) * slope[...]).astype(bf16)
    edge_gradient[...] = mm(grad, first_t[:, 2 * width :]).astype(bf16)
    at_receiver = mm(scatter_receive[...], grad) + mm(scatter_cut[...], cut)
    at_sender = mm(scatter_send[...], grad)
    total[...] = (
        jnp.where(valid, base[...], 0.0)
        + mm(at_receiver.astype(bf16), first_t[:, :width])
        + mm(at_sender.astype(bf16), first_t[:, width : 2 * width])
    )


def last_kernel(total, scatter_boundary, first_t, updated, edge_gradient, cut_gradient, *rest):
    arrived, outs, here, done = rest[:ROUNDS], rest[ROUNDS : ROUNDS + 4], *rest[ROUNDS + 4 :]
    held = (updated, edge_gradient, cut_gradient, here)
    copies = [pltpu.make_async_copy(a, b, done.at[i]) for i, (a, b) in enumerate(zip(held, outs))]
    for copy in copies[:3]:
        copy.start()
    width = total.shape[1]
    at_sender = mm(scatter_boundary[...], jnp.concatenate([a[...] for a in arrived], 0)).astype(bf16)
    here[...] = (total[...] + mm(at_sender, first_t[:, width : 2 * width])).astype(bf16)
    copies[3].start()
    for copy in copies:
        copy.wait()


VMEM = pl.BlockSpec(memory_space=pltpu.VMEM)
HBM = pl.BlockSpec(memory_space=pltpu.HBM)
SMEM = pl.BlockSpec(memory_space=pltpu.SMEM)


def call(kernel, out_shape, args, flops, held=(), scratch=(), written=0):
    size = sum(a.size * a.dtype.itemsize for a in args + tuple(held))
    return pl.pallas_call(
        kernel,
        out_shape=out_shape,
        in_specs=[SMEM if a.ndim == 1 else VMEM for a in args] + [HBM] * len(held),
        out_specs=[VMEM if i >= written else HBM for i in range(len(out_shape))],
        scratch_shapes=scratch,
        compiler_params=pltpu.CompilerParams(vmem_limit_bytes=32 * 1024 * 1024),
        cost_estimate=pl.CostEstimate(flops=flops, bytes_accessed=size if flops else 0, transcendentals=0),
    )(*args, *(pltpu.with_memory_space_constraint(a, pltpu.HBM) for a in held))


def shards(
    node_latent, edge_latent, cut_latent, node_cotangent, edge_sender, edge_receiver, boundary_rows,
    cut_slot, cut_receiver, node_count, edge_count, edge_first, edge_second, edge_gain, node_first,
    node_second, node_gain,
):
    nodes = node_latent[0]
    edges = edge_latent[0]
    cuts = cut_latent[0].reshape(-1, cut_latent.shape[-1])
    n, width = nodes.shape
    e, c = edges.shape[0], cuts.shape[0]
    boundary = boundary_rows.transpose(1, 0, 2)
    slot = cut_slot.transpose(1, 0, 2)
    cut_targets = cut_receiver.transpose(1, 0, 2)
    send = boundary.shape[2]
    shape = jax.ShapeDtypeStruct
    kept = pltpu.VMEM

    def copies(arrays):
        return [kept(a.shape, a.dtype) for a in arrays]

    held = (boundary, nodes, edge_receiver, edge_sender, slot, cut_targets, edge_gain[None], node_gain[None])
    outs = call(
        functools.partial(send_kernel, len(held)),
        copies(held) + [kept((send, width), bf16)] * ROUNDS,
        (),
        LONG,
        held,
        [pltpu.SemaphoreType.DMA((len(held),))],
    )
    boundary, nodes, edge_receiver, edge_sender, slot, cut_targets, edge_gain, node_gain = outs[: len(held)]
    sent = outs[len(held) :]
    arrived = exchange(sent)
    slots = ROUNDS * send
    some = -(-slots // 32) * 32
    all_slots = -(-slots // 128) * 128
    outs = call(
        inner_kernel,
        [
            kept((e, n), bf16), kept((e, width), f32), kept((e, 1), f32), kept((e, width), f32),
            kept((n, width), f32), kept((c, width), f32), kept((c, n), bf16), kept((c, all_slots), bf16),
            kept((n, e), bf16), kept((n, e), bf16), kept((n, c), bf16), kept((some, c), bf16),
            kept((n, slots), bf16), kept((width, 3 * width), bf16), kept((width, width), bf16),
        ],
        (
            edge_count, nodes, edges, cuts, edge_sender, edge_receiver, slot, cut_targets, boundary, edge_first,
            edge_second,
        ),
        LONG,
    )
    gather, normed, inverse, slope, received, near, gather_cut, gather_far = outs[:8]
    scatter_receive, scatter_send, scatter_cut, scatter_far, scatter_boundary, first_t, second_t = outs[8:]
    outs = call(
        main_kernel,
        [kept((n, width), bf16), kept((n, width), f32), kept((2 * n, width), bf16), kept((c, width), bf16)]
        + [kept((send, width), bf16)] * ROUNDS,
        (
            nodes, node_cotangent[0], edge_first, edge_second, edge_gain, node_first, node_second, node_gain,
            received, near, gather_cut, gather_far, scatter_cut, scatter_far, second_t, *arrived,
        ),
        2 * c * width * width * 6,
    )
    updated, base, gained, grad_cut = outs[:4]
    returned = exchange(outs[4:])
    updated, edge_gradient, cut_gradient, total = call(
        outer_kernel,
        [kept((n, width), bf16), kept((e, width), bf16), kept((c, width), bf16), kept((n, width), f32)],
        (
            node_count, gained, gather, normed, inverse, slope, first_t, second_t, scatter_receive, scatter_send,
            scatter_cut, grad_cut, base, updated,
        ),
        0,
    )
    updated, edge_gradient, cut_gradient, node_gradient = call(
        last_kernel,
        [shape((n, width), bf16), shape((e, width), bf16), shape((c, width), bf16), shape((n, width), bf16)],
        (total, scatter_boundary, first_t, updated, edge_gradient, cut_gradient, *returned),
        2 * 2 * n * width * width,
        scratch=[pltpu.VMEM((n, width), bf16), pltpu.SemaphoreType.DMA((4,))],
        written=4,
    )
    return (
        updated[None],
        node_gradient[None],
        edge_gradient[None],
        cut_gradient.reshape(cut_latent.shape),
    )


def solution(mesh):
    part = ("grp", "dev")
    placed = tuple(P(part, *[None] * (d - 1)) for d in (3, 3, 4, 3, 2, 2, 3, 3, 3, 1, 1)) + (P(),) * 6
    return jax.shard_map(
        shards,
        mesh=mesh,
        in_specs=placed,
        out_specs=tuple(P(part, *[None] * (d - 1)) for d in (3, 3, 3, 4)),
        check_vma=False,
    )
```

```python
import functools

import jax
import jax.numpy as jnp
from jax import lax
from jax.experimental import pallas as pl
from jax.experimental.pallas import tpu as pltpu
from jax.sharding import PartitionSpec as P

ROUNDS = 5
GRP_ROUNDS = 2
LONG = 4 * 10**9

epsilon = 1e-05

bf16 = jnp.bfloat16
f32 = jnp.float32


def partner(shard, round_index):
    axis, apart = ("grp", round_index) if round_index < GRP_ROUNDS else ("dev", round_index - GRP_ROUNDS)
    return lax.ppermute(shard, axis, [(i, i ^ 1 << apart) for i in range(lax.axis_size(axis))])


def exchange(rows):
    got = lax.optimization_barrier([partner(rows[r], r) for r in reversed(range(ROUNDS))])
    return got[::-1]


def mm(a, b):
    return jnp.dot(a, b, preferred_element_type=f32)


def mm_t(a, b):
    return lax.dot_general(a, b, (((1,), (1,)), ((), ())), preferred_element_type=f32)


def hot(row, count):
    shape = (count, row.shape[1])
    return (lax.broadcasted_iota(jnp.int32, shape, 0) == jnp.broadcast_to(row, shape)).astype(f32)


def split(values):
    high = values.astype(bf16)
    return high, (values - high.astype(f32)).astype(bf16)


def add_rows(table, values):
    return mm(jnp.concatenate([table, table], 1), jnp.concatenate(split(values), 0))


def lane_mean(values):
    return jnp.mean(values, axis=-1, keepdims=True)


def norm_parts(values):
    centred = values - lane_mean(values)
    inverse = lax.rsqrt(lane_mean(centred * centred) + epsilon)
    return centred * inverse, inverse


def centred_parts(weights):
    values = weights.astype(f32)
    return jnp.concatenate(split(values - lane_mean(values)), 0)


def norm_centred(act, parts):
    centred = mm(jnp.concatenate([act, act], 1), parts)
    inverse = lax.rsqrt(lane_mean(centred * centred) + epsilon)
    return centred * inverse, inverse


def norm_backward(scaled, normed, inverse):
    return inverse * (scaled - lane_mean(scaled) - normed * lane_mean(scaled * normed))


def silu_parts(values):
    sigmoid = jax.nn.sigmoid(values)
    act = values * sigmoid
    return act, sigmoid + act * (1.0 - sigmoid)


def load(held, loaded, done):
    copies = [pltpu.make_async_copy(h, v, done.at[i]) for i, (h, v) in enumerate(zip(held, loaded))]
    for copy in copies:
        copy.start()
    return copies


def send_kernel(count, *rest):
    held, loaded, out, done = rest[:count], rest[count : 2 * count], rest[2 * count : -1], rest[-1]
    copies = load(held, loaded, done)
    boundary, nodes = loaded[:2]
    copies[0].wait()
    table = jnp.concatenate([hot(boundary[r], nodes.shape[0]) for r in range(ROUNDS)], 1).T.astype(bf16)
    copies[1].wait()
    rows = mm(table, nodes[...]).astype(bf16)
    send = boundary.shape[2]
    for r in range(ROUNDS):
        out[r][...] = rows[r * send : (r + 1) * send]
    for copy in copies[2:]:
        copy.wait()


def inner_kernel(
    edge_count, nodes, edges, cuts, sender, receiver, slot, cut_receiver, boundary, edge_first, edge_second,
    gather_out, normed_out, inverse_out, slope_out, received, near, gather_cut, gather_far,
    scatter_receive, scatter_send, scatter_cut, scatter_far, scatter_boundary, first_t, second_t,
    second_centred,
):
    n, width = nodes.shape
    e = edges.shape[0]
    used = lax.broadcasted_iota(jnp.int32, (1, e), 1) < edge_count[0]
    hot_receive = hot(jnp.where(used, receiver[...], -1), n)
    hot_send = hot(sender[...], n)
    hot_cut = jnp.concatenate([hot(cut_receiver[r], n) for r in range(ROUNDS)], 1)
    gather = jnp.concatenate([hot_receive, hot_send, hot_cut], 1).T.astype(bf16)
    ends = mm(gather, nodes[...]).astype(bf16)
    pre = mm(jnp.concatenate([ends[:e], ends[e : 2 * e], edges[...]], 1), edge_first[...])
    act, slope = silu_parts(pre)
    normed, inverse = norm_parts(mm(act.astype(bf16), edge_second[...]))
    gather_out[...] = gather[:e]
    normed_out[...] = normed
    inverse_out[...] = inverse
    slope_out[...] = slope
    received[...] = add_rows(hot_receive.astype(bf16), normed)
    scatter_receive[...] = hot_receive.astype(bf16)
    scatter_send[...] = hot_send.astype(bf16)

    send = boundary.shape[2]
    hot_far = hot(jnp.concatenate([slot[r] + r * send for r in range(ROUNDS)], 1), gather_far.shape[1])
    near[...] = mm(ends[2 * e :], edge_first[:width]) + mm(cuts[...], edge_first[2 * width :])
    gather_cut[...] = gather[2 * e :]
    gather_far[...] = hot_far.T.astype(bf16)
    scatter_cut[...] = hot_cut.astype(bf16)
    scatter_far[...] = hot_far[: scatter_far.shape[0]].astype(bf16)
    scatter_boundary[...] = jnp.concatenate([hot(boundary[r], n) for r in range(ROUNDS)], 1).astype(bf16)
    first_t[...] = edge_first[...].T
    second_t[...] = edge_second[...].T
    second_centred[...] = centred_parts(edge_second[...])


def main_kernel(
    nodes, cotangent, edge_first, second_centred, edge_gain, node_first, node_second, node_gain, received_inner, near,
    gather_cut, gather_far, scatter_cut, scatter_far, second_t, *rest,
):
    arrived = rest[:ROUNDS]
    updated, base, grad_nodes, grad_cut = rest[ROUNDS : ROUNDS + 4]
    back = rest[ROUNDS + 4 :]
    n, width = nodes.shape
    send = arrived[0].shape[0]
    x = nodes[...]
    empty = jnp.zeros((gather_far.shape[1] - ROUNDS * send, width), bf16)
    far = jnp.concatenate([a[...] for a in arrived] + [empty], 0)
    far_end = mm(gather_far[...], far).astype(bf16)
    pre = near[...] + mm(far_end, edge_first[width : 2 * width])
    act, slope = silu_parts(pre)
    normed, inverse = norm_centred(act.astype(bf16), second_centred[...])
    received = (received_inner[...] + add_rows(scatter_cut[...], normed)) * edge_gain[...]

    pre_node = mm(jnp.concatenate([x, received.astype(bf16)], 1), node_first[...])
    act_node, slope_node = silu_parts(pre_node)
    normed_node, inverse_node = norm_centred(act_node.astype(bf16), centred_parts(node_second[...]))
    updated[...] = (x.astype(f32) + normed_node * node_gain[...]).astype(bf16)
    upstream = cotangent[...].astype(f32)
    grad_out_node = norm_backward(upstream * node_gain[...], normed_node, inverse_node).astype(bf16)
    grad_pre_node = (mm_t(grad_out_node, node_second[...]) * slope_node).astype(bf16)
    gathered = mm(gather_cut[...], grad_pre_node).astype(bf16)
    scaled = mm_t(gathered, node_first[width:]) * edge_gain[...]
    grad_out = norm_backward(scaled, normed, inverse).astype(bf16)
    grad = (mm(grad_out, second_t[...]) * slope).astype(bf16)
    sums = mm(scatter_far[...], grad).astype(bf16)
    for r in range(ROUNDS):
        back[r][...] = sums[r * send : (r + 1) * send]
    grad_cut[...] = grad
    grad_nodes[...] = grad_pre_node
    base[...] = upstream + mm_t(grad_pre_node, node_first[:width])


def outer_kernel(
    node_count, grad_nodes, node_first, edge_gain, gather, normed, inverse, slope, first_t, second_t, scatter_receive, scatter_send, scatter_cut,
    grad_cut, base, updated_in, updated, edge_gradient, cut_gradient, total,
):
    n, width = base.shape
    valid = lax.broadcasted_iota(jnp.int32, (n, width), 0) < node_count[0]
    updated[...] = jnp.where(valid, updated_in[...].astype(f32), 0.0).astype(bf16)
    cut = grad_cut[...]
    cut_gradient[...] = mm(cut, first_t[:, 2 * width :]).astype(bf16)
    gathered = mm(gather[...], grad_nodes[...]).astype(bf16)
    scaled = mm_t(gathered, node_first[width:]) * edge_gain[...]
    grad_out = norm_backward(scaled, normed[...], inverse[...]).astype(bf16)
    grad = (mm(grad_out, second_t[...]) * slope[...]).astype(bf16)
    edge_gradient[...] = mm(grad, first_t[:, 2 * width :]).astype(bf16)
    at_receiver = mm(scatter_receive[...], grad) + mm(scatter_cut[...], cut)
    at_sender = mm(scatter_send[...], grad)
    total[...] = (
        jnp.where(valid, base[...], 0.0)
        + mm(at_receiver.astype(bf16), first_t[:, :width])
        + mm(at_sender.astype(bf16), first_t[:, width : 2 * width])
    )


def last_kernel(total, scatter_boundary, first_t, updated, edge_gradient, cut_gradient, *rest):
    arrived, outs, here, done = rest[:ROUNDS], rest[ROUNDS : ROUNDS + 4], *rest[ROUNDS + 4 :]
    held = (updated, edge_gradient, cut_gradient, here)
    copies = [pltpu.make_async_copy(a, b, done.at[i]) for i, (a, b) in enumerate(zip(held, outs))]
    for copy in copies[:3]:
        copy.start()
    width = total.shape[1]
    at_sender = mm(scatter_boundary[...], jnp.concatenate([a[...] for a in arrived], 0)).astype(bf16)
    here[...] = (total[...] + mm(at_sender, first_t[:, width : 2 * width])).astype(bf16)
    copies[3].start()
    for copy in copies:
        copy.wait()


VMEM = pl.BlockSpec(memory_space=pltpu.VMEM)
HBM = pl.BlockSpec(memory_space=pltpu.HBM)
SMEM = pl.BlockSpec(memory_space=pltpu.SMEM)


def call(kernel, out_shape, args, flops, held=(), scratch=(), written=0):
    size = sum(a.size * a.dtype.itemsize for a in args + tuple(held))
    return pl.pallas_call(
        kernel,
        out_shape=out_shape,
        in_specs=[SMEM if a.ndim == 1 else VMEM for a in args] + [HBM] * len(held),
        out_specs=[VMEM if i >= written else HBM for i in range(len(out_shape))],
        scratch_shapes=scratch,
        compiler_params=pltpu.CompilerParams(vmem_limit_bytes=32 * 1024 * 1024),
        cost_estimate=pl.CostEstimate(flops=flops, bytes_accessed=size if flops else 0, transcendentals=0),
    )(*args, *(pltpu.with_memory_space_constraint(a, pltpu.HBM) for a in held))


def shards(
    node_latent, edge_latent, cut_latent, node_cotangent, edge_sender, edge_receiver, boundary_rows,
    cut_slot, cut_receiver, node_count, edge_count, edge_first, edge_second, edge_gain, node_first,
    node_second, node_gain,
):
    nodes = node_latent[0]
    edges = edge_latent[0]
    cuts = cut_latent[0].reshape(-1, cut_latent.shape[-1])
    n, width = nodes.shape
    e, c = edges.shape[0], cuts.shape[0]
    boundary = boundary_rows.transpose(1, 0, 2)
    slot = cut_slot.transpose(1, 0, 2)
    cut_targets = cut_receiver.transpose(1, 0, 2)
    send = boundary.shape[2]
    shape = jax.ShapeDtypeStruct
    kept = pltpu.VMEM

    def copies(arrays):
        return [kept(a.shape, a.dtype) for a in arrays]

    held = (boundary, nodes, edge_receiver, edge_sender, slot, cut_targets, edge_gain[None], node_gain[None])
    outs = call(
        functools.partial(send_kernel, len(held)),
        copies(held) + [kept((send, width), bf16)] * ROUNDS,
        (),
        LONG,
        held,
        [pltpu.SemaphoreType.DMA((len(held),))],
    )
    boundary, nodes, edge_receiver, edge_sender, slot, cut_targets, edge_gain, node_gain = outs[: len(held)]
    sent = outs[len(held) :]
    arrived = exchange(sent)
    slots = ROUNDS * send
    some = -(-slots // 32) * 32
    all_slots = -(-slots // 128) * 128
    outs = call(
        inner_kernel,
        [
            kept((e, n), bf16), kept((e, width), f32), kept((e, 1), f32), kept((e, width), f32),
            kept((n, width), f32), kept((c, width), f32), kept((c, n), bf16), kept((c, all_slots), bf16),
            kept((n, e), bf16), kept((n, e), bf16), kept((n, c), bf16), kept((some, c), bf16),
            kept((n, slots), bf16), kept((width, 3 * width), bf16), kept((width, width), bf16),
            kept((2 * width, width), bf16),
        ],
        (
            edge_count, nodes, edges, cuts, edge_sender, edge_receiver, slot, cut_targets, boundary, edge_first,
            edge_second,
        ),
        LONG,
    )
    gather, normed, inverse, slope, received, near, gather_cut, gather_far = outs[:8]
    scatter_receive, scatter_send, scatter_cut, scatter_far, scatter_boundary, first_t, second_t, second_centred = outs[8:]
    outs = call(
        main_kernel,
        [kept((n, width), bf16), kept((n, width), f32), kept((n, width), bf16), kept((c, width), bf16)]
        + [kept((send, width), bf16)] * ROUNDS,
        (
            nodes, node_cotangent[0], edge_first, second_centred, edge_gain, node_first, node_second, node_gain,
            received, near, gather_cut, gather_far, scatter_cut, scatter_far, second_t, *arrived,
        ),
        2 * c * width * width * 6,
    )
    updated, base, grad_nodes, grad_cut = outs[:4]
    returned = exchange(outs[4:])
    updated, edge_gradient, cut_gradient, total = call(
        outer_kernel,
        [kept((n, width), bf16), kept((e, width), bf16), kept((c, width), bf16), kept((n, width), f32)],
        (
            node_count, grad_nodes, node_first, edge_gain, gather, normed, inverse, slope, first_t, second_t, scatter_receive, scatter_send,
            scatter_cut, grad_cut, base, updated,
        ),
        0,
    )
    updated, edge_gradient, cut_gradient, node_gradient = call(
        last_kernel,
        [shape((n, width), bf16), shape((e, width), bf16), shape((c, width), bf16), shape((n, width), bf16)],
        (total, scatter_boundary, first_t, updated, edge_gradient, cut_gradient, *returned),
        2 * 2 * n * width * width,
        scratch=[pltpu.VMEM((n, width), bf16), pltpu.SemaphoreType.DMA((4,))],
        written=4,
    )
    return (
        updated[None],
        node_gradient[None],
        edge_gradient[None],
        cut_gradient.reshape(cut_latent.shape),
    )


def solution(mesh):
    part = ("grp", "dev")
    placed = tuple(P(part, *[None] * (d - 1)) for d in (3, 3, 4, 3, 2, 2, 3, 3, 3, 1, 1)) + (P(),) * 6
    return jax.shard_map(
        shards,
        mesh=mesh,
        in_specs=placed,
        out_specs=tuple(P(part, *[None] * (d - 1)) for d in (3, 3, 3, 4)),
        check_vma=False,
    )
```

```python
import functools

import jax
import jax.numpy as jnp
from jax import lax
from jax.experimental import pallas as pl
from jax.experimental.pallas import tpu as pltpu
from jax.sharding import PartitionSpec as P

ROUNDS = 5
GRP_ROUNDS = 2
LONG = 4 * 10**9

epsilon = 1e-05

bf16 = jnp.bfloat16
f32 = jnp.float32


def partner(shard, round_index):
    axis, apart = ("grp", round_index) if round_index < GRP_ROUNDS else ("dev", round_index - GRP_ROUNDS)
    return lax.ppermute(shard, axis, [(i, i ^ 1 << apart) for i in range(lax.axis_size(axis))])


def exchange(rows):
    got = lax.optimization_barrier([partner(rows[r], r) for r in reversed(range(ROUNDS))])
    return got[::-1]


def mm(a, b):
    return jnp.dot(a, b, preferred_element_type=f32)


def mm_t(a, b):
    return lax.dot_general(a, b, (((1,), (1,)), ((), ())), preferred_element_type=f32)


def hot(row, count):
    shape = (count, row.shape[1])
    return (lax.broadcasted_iota(jnp.int32, shape, 0) == jnp.broadcast_to(row, shape)).astype(f32)


def split(values):
    high = values.astype(bf16)
    return high, (values - high.astype(f32)).astype(bf16)


def add_rows(table, values):
    return mm(jnp.concatenate([table, table], 1), jnp.concatenate(split(values), 0))


def lane_mean(values):
    return jnp.mean(values, axis=-1, keepdims=True)


def norm_parts(values):
    centred = values - lane_mean(values)
    inverse = lax.rsqrt(lane_mean(centred * centred) + epsilon)
    return centred * inverse, inverse


def centred_parts(weights):
    values = weights.astype(f32)
    return jnp.concatenate(split(values - lane_mean(values)), 0)


def norm_centred(act, parts):
    centred = mm(jnp.concatenate([act, act], 1), parts)
    inverse = lax.rsqrt(lane_mean(centred * centred) + epsilon)
    return centred * inverse, inverse


def norm_backward(scaled, normed, inverse):
    return inverse * (scaled - lane_mean(scaled) - normed * lane_mean(scaled * normed))


def silu_parts(values):
    sigmoid = jax.nn.sigmoid(values)
    act = values * sigmoid
    return act, sigmoid + act * (1.0 - sigmoid)


def load(held, loaded, done):
    copies = [pltpu.make_async_copy(h, v, done.at[i]) for i, (h, v) in enumerate(zip(held, loaded))]
    for copy in copies:
        copy.start()
    return copies


def send_kernel(count, *rest):
    held, loaded, out, done = rest[:count], rest[count : 2 * count], rest[2 * count : -1], rest[-1]
    copies = load(held, loaded, done)
    boundary, nodes = loaded[:2]
    copies[0].wait()
    table = jnp.concatenate([hot(boundary[r], nodes.shape[0]) for r in range(ROUNDS)], 1).T.astype(bf16)
    copies[1].wait()
    rows = mm(table, nodes[...]).astype(bf16)
    send = boundary.shape[2]
    for r in range(ROUNDS):
        out[r][...] = rows[r * send : (r + 1) * send]
    for copy in copies[2:]:
        copy.wait()


def inner_kernel(
    edge_count, nodes, edges, cuts, sender, receiver, slot, cut_receiver, boundary, edge_first, edge_second,
    gather_out, normed_out, inverse_out, slope_out, received, near, gather_cut, gather_far,
    scatter_receive, scatter_send, scatter_cut, scatter_far, scatter_boundary, first_t, second_t,
    second_centred,
):
    n, width = nodes.shape
    e = edges.shape[0]
    used = lax.broadcasted_iota(jnp.int32, (1, e), 1) < edge_count[0]
    hot_receive = hot(jnp.where(used, receiver[...], -1), n)
    hot_send = hot(sender[...], n)
    hot_cut = jnp.concatenate([hot(cut_receiver[r], n) for r in range(ROUNDS)], 1)
    gather = jnp.concatenate([hot_receive, hot_send, hot_cut], 1).T.astype(bf16)
    ends = mm(gather, nodes[...]).astype(bf16)
    pre = mm(jnp.concatenate([ends[:e], ends[e : 2 * e], edges[...]], 1), edge_first[...])
    act, slope = silu_parts(pre)
    normed, inverse = norm_parts(mm(act.astype(bf16), edge_second[...]))
    gather_out[...] = gather[:e]
    normed_out[...] = normed
    inverse_out[...] = inverse
    slope_out[...] = slope
    received[...] = add_rows(hot_receive.astype(bf16), normed)
    scatter_receive[...] = hot_receive.astype(bf16)
    scatter_send[...] = hot_send.astype(bf16)

    send = boundary.shape[2]
    hot_far = hot(jnp.concatenate([slot[r] + r * send for r in range(ROUNDS)], 1), gather_far.shape[1])
    near[...] = mm(ends[2 * e :], edge_first[:width]) + mm(cuts[...], edge_first[2 * width :])
    gather_cut[...] = gather[2 * e :]
    gather_far[...] = hot_far.T.astype(bf16)
    scatter_cut[...] = hot_cut.astype(bf16)
    scatter_far[...] = hot_far[: scatter_far.shape[0]].astype(bf16)
    scatter_boundary[...] = jnp.concatenate([hot(boundary[r], n) for r in range(ROUNDS)], 1).astype(bf16)
    first_t[...] = edge_first[...].T
    second_t[...] = edge_second[...].T
    second_centred[...] = centred_parts(edge_second[...])


def main_kernel(
    nodes, cotangent, edge_first, second_centred, edge_gain, node_first, node_second, node_gain, received_inner, near,
    gather_cut, gather_far, scatter_cut, scatter_far, second_t, *rest,
):
    arrived = rest[:ROUNDS]
    updated, grad_nodes, grad_cut = rest[ROUNDS : ROUNDS + 3]
    back = rest[ROUNDS + 3 :]
    n, width = nodes.shape
    send = arrived[0].shape[0]
    x = nodes[...]
    empty = jnp.zeros((gather_far.shape[1] - ROUNDS * send, width), bf16)
    far = jnp.concatenate([a[...] for a in arrived] + [empty], 0)
    far_end = mm(gather_far[...], far).astype(bf16)
    pre = near[...] + mm(far_end, edge_first[width : 2 * width])
    act, slope = silu_parts(pre)
    normed, inverse = norm_centred(act.astype(bf16), second_centred[...])
    received = (received_inner[...] + add_rows(scatter_cut[...], normed)) * edge_gain[...]

    pre_node = mm(jnp.concatenate([x, received.astype(bf16)], 1), node_first[...])
    act_node, slope_node = silu_parts(pre_node)
    normed_node, inverse_node = norm_centred(act_node.astype(bf16), centred_parts(node_second[...]))
    updated[...] = (x.astype(f32) + normed_node * node_gain[...]).astype(bf16)
    upstream = cotangent[...].astype(f32)
    grad_out_node = norm_backward(upstream * node_gain[...], normed_node, inverse_node).astype(bf16)
    grad_pre_node = (mm_t(grad_out_node, node_second[...]) * slope_node).astype(bf16)
    gathered = mm(gather_cut[...], grad_pre_node).astype(bf16)
    scaled = mm_t(gathered, node_first[width:]) * edge_gain[...]
    grad_out = norm_backward(scaled, normed, inverse).astype(bf16)
    grad = (mm(grad_out, second_t[...]) * slope).astype(bf16)
    sums = mm(scatter_far[...], grad).astype(bf16)
    for r in range(ROUNDS):
        back[r][...] = sums[r * send : (r + 1) * send]
    grad_cut[...] = grad
    grad_nodes[...] = grad_pre_node


def outer_kernel(
    node_count, grad_nodes, node_first, edge_gain, gather, normed, inverse, slope, first_t, second_t, scatter_receive, scatter_send, scatter_cut,
    grad_cut, cotangent, updated_in, updated, edge_gradient, cut_gradient, total,
):
    n, width = cotangent.shape
    valid = lax.broadcasted_iota(jnp.int32, (n, width), 0) < node_count[0]
    updated[...] = jnp.where(valid, updated_in[...].astype(f32), 0.0).astype(bf16)
    cut = grad_cut[...]
    cut_gradient[...] = mm(cut, first_t[:, 2 * width :]).astype(bf16)
    gathered = mm(gather[...], grad_nodes[...]).astype(bf16)
    scaled = mm_t(gathered, node_first[width:]) * edge_gain[...]
    grad_out = norm_backward(scaled, normed[...], inverse[...]).astype(bf16)
    grad = (mm(grad_out, second_t[...]) * slope[...]).astype(bf16)
    edge_gradient[...] = mm(grad, first_t[:, 2 * width :]).astype(bf16)
    at_receiver = mm(scatter_receive[...], grad) + mm(scatter_cut[...], cut)
    at_sender = mm(scatter_send[...], grad)
    total[...] = (
        jnp.where(valid, cotangent[...].astype(f32) + mm_t(grad_nodes[...], node_first[:width]), 0.0)
        + mm(at_receiver.astype(bf16), first_t[:, :width])
        + mm(at_sender.astype(bf16), first_t[:, width : 2 * width])
    )


def last_kernel(total, scatter_boundary, first_t, updated, edge_gradient, cut_gradient, *rest):
    arrived, outs, here, done = rest[:ROUNDS], rest[ROUNDS : ROUNDS + 4], *rest[ROUNDS + 4 :]
    held = (updated, edge_gradient, cut_gradient, here)
    copies = [pltpu.make_async_copy(a, b, done.at[i]) for i, (a, b) in enumerate(zip(held, outs))]
    for copy in copies[:3]:
        copy.start()
    width = total.shape[1]
    at_sender = mm(scatter_boundary[...], jnp.concatenate([a[...] for a in arrived], 0)).astype(bf16)
    here[...] = (total[...] + mm(at_sender, first_t[:, width : 2 * width])).astype(bf16)
    copies[3].start()
    for copy in copies:
        copy.wait()


VMEM = pl.BlockSpec(memory_space=pltpu.VMEM)
HBM = pl.BlockSpec(memory_space=pltpu.HBM)
SMEM = pl.BlockSpec(memory_space=pltpu.SMEM)


def call(kernel, out_shape, args, flops, held=(), scratch=(), written=0):
    size = sum(a.size * a.dtype.itemsize for a in args + tuple(held))
    return pl.pallas_call(
        kernel,
        out_shape=out_shape,
        in_specs=[SMEM if a.ndim == 1 else VMEM for a in args] + [HBM] * len(held),
        out_specs=[VMEM if i >= written else HBM for i in range(len(out_shape))],
        scratch_shapes=scratch,
        compiler_params=pltpu.CompilerParams(vmem_limit_bytes=32 * 1024 * 1024),
        cost_estimate=pl.CostEstimate(flops=flops, bytes_accessed=size if flops else 0, transcendentals=0),
    )(*args, *(pltpu.with_memory_space_constraint(a, pltpu.HBM) for a in held))


def shards(
    node_latent, edge_latent, cut_latent, node_cotangent, edge_sender, edge_receiver, boundary_rows,
    cut_slot, cut_receiver, node_count, edge_count, edge_first, edge_second, edge_gain, node_first,
    node_second, node_gain,
):
    nodes = node_latent[0]
    edges = edge_latent[0]
    cuts = cut_latent[0].reshape(-1, cut_latent.shape[-1])
    n, width = nodes.shape
    e, c = edges.shape[0], cuts.shape[0]
    boundary = boundary_rows.transpose(1, 0, 2)
    slot = cut_slot.transpose(1, 0, 2)
    cut_targets = cut_receiver.transpose(1, 0, 2)
    send = boundary.shape[2]
    shape = jax.ShapeDtypeStruct
    kept = pltpu.VMEM

    def copies(arrays):
        return [kept(a.shape, a.dtype) for a in arrays]

    held = (boundary, nodes, edge_receiver, edge_sender, slot, cut_targets, edge_gain[None], node_gain[None])
    outs = call(
        functools.partial(send_kernel, len(held)),
        copies(held) + [kept((send, width), bf16)] * ROUNDS,
        (),
        LONG,
        held,
        [pltpu.SemaphoreType.DMA((len(held),))],
    )
    boundary, nodes, edge_receiver, edge_sender, slot, cut_targets, edge_gain, node_gain = outs[: len(held)]
    sent = outs[len(held) :]
    arrived = exchange(sent)
    slots = ROUNDS * send
    some = -(-slots // 32) * 32
    all_slots = -(-slots // 128) * 128
    outs = call(
        inner_kernel,
        [
            kept((e, n), bf16), kept((e, width), f32), kept((e, 1), f32), kept((e, width), f32),
            kept((n, width), f32), kept((c, width), f32), kept((c, n), bf16), kept((c, all_slots), bf16),
            kept((n, e), bf16), kept((n, e), bf16), kept((n, c), bf16), kept((some, c), bf16),
            kept((n, slots), bf16), kept((width, 3 * width), bf16), kept((width, width), bf16),
            kept((2 * width, width), bf16),
        ],
        (
            edge_count, nodes, edges, cuts, edge_sender, edge_receiver, slot, cut_targets, boundary, edge_first,
            edge_second,
        ),
        LONG,
    )
    gather, normed, inverse, slope, received, near, gather_cut, gather_far = outs[:8]
    scatter_receive, scatter_send, scatter_cut, scatter_far, scatter_boundary, first_t, second_t, second_centred = outs[8:]
    outs = call(
        main_kernel,
        [kept((n, width), bf16), kept((n, width), bf16), kept((c, width), bf16)]
        + [kept((send, width), bf16)] * ROUNDS,
        (
            nodes, node_cotangent[0], edge_first, second_centred, edge_gain, node_first, node_second, node_gain,
            received, near, gather_cut, gather_far, scatter_cut, scatter_far, second_t, *arrived,
        ),
        2 * c * width * width * 6,
    )
    updated, grad_nodes, grad_cut = outs[:3]
    returned = exchange(outs[3:])
    updated, edge_gradient, cut_gradient, total = call(
        outer_kernel,
        [kept((n, width), bf16), kept((e, width), bf16), kept((c, width), bf16), kept((n, width), f32)],
        (
            node_count, grad_nodes, node_first, edge_gain, gather, normed, inverse, slope, first_t, second_t, scatter_receive, scatter_send,
            scatter_cut, grad_cut, node_cotangent[0], updated,
        ),
        0,
    )
    updated, edge_gradient, cut_gradient, node_gradient = call(
        last_kernel,
        [shape((n, width), bf16), shape((e, width), bf16), shape((c, width), bf16), shape((n, width), bf16)],
        (total, scatter_boundary, first_t, updated, edge_gradient, cut_gradient, *returned),
        2 * 2 * n * width * width,
        scratch=[pltpu.VMEM((n, width), bf16), pltpu.SemaphoreType.DMA((4,))],
        written=4,
    )
    return (
        updated[None],
        node_gradient[None],
        edge_gradient[None],
        cut_gradient.reshape(cut_latent.shape),
    )


def solution(mesh):
    part = ("grp", "dev")
    placed = tuple(P(part, *[None] * (d - 1)) for d in (3, 3, 4, 3, 2, 2, 3, 3, 3, 1, 1)) + (P(),) * 6
    return jax.shard_map(
        shards,
        mesh=mesh,
        in_specs=placed,
        out_specs=tuple(P(part, *[None] * (d - 1)) for d in (3, 3, 3, 4)),
        check_vma=False,
    )
```

```python
import functools

import jax
import jax.numpy as jnp
from jax import lax
from jax.experimental import pallas as pl
from jax.experimental.pallas import tpu as pltpu
from jax.sharding import PartitionSpec as P

ROUNDS = 5
GRP_ROUNDS = 2
LONG = 4 * 10**9

epsilon = 1e-05

bf16 = jnp.bfloat16
f32 = jnp.float32


def partner(shard, round_index):
    axis, apart = ("grp", round_index) if round_index < GRP_ROUNDS else ("dev", round_index - GRP_ROUNDS)
    return lax.ppermute(shard, axis, [(i, i ^ 1 << apart) for i in range(lax.axis_size(axis))])


def exchange(rows):
    got = lax.optimization_barrier([partner(rows[r], r) for r in reversed(range(ROUNDS))])
    return got[::-1]


def mm(a, b):
    return jnp.dot(a, b, preferred_element_type=f32)


def mm_t(a, b):
    return lax.dot_general(a, b, (((1,), (1,)), ((), ())), preferred_element_type=f32)


def hot(row, count):
    shape = (count, row.shape[1])
    return (lax.broadcasted_iota(jnp.int32, shape, 0) == jnp.broadcast_to(row, shape)).astype(f32)


def split(values):
    high = values.astype(bf16)
    return high, (values - high.astype(f32)).astype(bf16)


def add_rows(table, values):
    return mm(jnp.concatenate([table, table], 1), jnp.concatenate(split(values), 0))


def lane_mean(values):
    return jnp.mean(values, axis=-1, keepdims=True)


def norm_parts(values):
    centred = values - lane_mean(values)
    inverse = lax.rsqrt(lane_mean(centred * centred) + epsilon)
    return centred * inverse, inverse


def centred_parts(weights):
    values = weights.astype(f32)
    return jnp.concatenate(split(values - lane_mean(values)), 0)


def norm_centred(act, parts):
    centred = mm(jnp.concatenate([act, act], 1), parts)
    inverse = lax.rsqrt(lane_mean(centred * centred) + epsilon)
    return centred * inverse, inverse


def norm_backward(scaled, normed, inverse):
    return inverse * (scaled - lane_mean(scaled) - normed * lane_mean(scaled * normed))


def silu_parts(values):
    sigmoid = jax.nn.sigmoid(values)
    act = values * sigmoid
    return act, sigmoid + act * (1.0 - sigmoid)


def load(held, loaded, done):
    copies = [pltpu.make_async_copy(h, v, done.at[i]) for i, (h, v) in enumerate(zip(held, loaded))]
    for copy in copies:
        copy.start()
    return copies


def send_kernel(count, *rest):
    held, loaded, out, done = rest[:count], rest[count : 2 * count], rest[2 * count : -1], rest[-1]
    copies = load(held, loaded, done)
    boundary, nodes = loaded[:2]
    copies[0].wait()
    table = jnp.concatenate([hot(boundary[r], nodes.shape[0]) for r in range(ROUNDS)], 1).T.astype(bf16)
    copies[1].wait()
    rows = mm(table, nodes[...]).astype(bf16)
    send = boundary.shape[2]
    for r in range(ROUNDS):
        out[r][...] = rows[r * send : (r + 1) * send]
    for copy in copies[2:]:
        copy.wait()


def inner_kernel(
    edge_count, nodes, edges, cuts, sender, receiver, slot, cut_receiver, boundary, edge_first, edge_second,
    gather_out, normed_out, inverse_out, slope_out, received, near, gather_cut, gather_far,
    scatter_receive, scatter_send, scatter_cut, scatter_far, scatter_boundary, first_t, second_t,
    second_centred,
):
    n, width = nodes.shape
    e = edges.shape[0]
    used = lax.broadcasted_iota(jnp.int32, (1, e), 1) < edge_count[0]
    hot_receive = hot(jnp.where(used, receiver[...], -1), n)
    hot_send = hot(sender[...], n)
    hot_cut = jnp.concatenate([hot(cut_receiver[r], n) for r in range(ROUNDS)], 1)
    gather = jnp.concatenate([hot_receive, hot_send, hot_cut], 1).T.astype(bf16)
    ends = mm(gather, nodes[...]).astype(bf16)
    pre = mm(jnp.concatenate([ends[:e], ends[e : 2 * e], edges[...]], 1), edge_first[...])
    act, slope = silu_parts(pre)
    normed, inverse = norm_parts(mm(act.astype(bf16), edge_second[...]))
    gather_out[...] = gather[:e]
    normed_out[...] = normed
    inverse_out[...] = inverse
    slope_out[...] = slope
    received[...] = add_rows(hot_receive.astype(bf16), normed)
    scatter_receive[...] = hot_receive.astype(bf16)
    scatter_send[...] = hot_send.astype(bf16)

    send = boundary.shape[2]
    hot_far = hot(jnp.concatenate([slot[r] + r * send for r in range(ROUNDS)], 1), gather_far.shape[1])
    near[...] = mm(ends[2 * e :], edge_first[:width]) + mm(cuts[...], edge_first[2 * width :])
    gather_cut[...] = gather[2 * e :]
    gather_far[...] = hot_far.T.astype(bf16)
    scatter_cut[...] = hot_cut.astype(bf16)
    scatter_far[...] = hot_far[: scatter_far.shape[0]].astype(bf16)
    scatter_boundary[...] = jnp.concatenate([hot(boundary[r], n) for r in range(ROUNDS)], 1).astype(bf16)
    first_t[...] = edge_first[...].T
    second_t[...] = edge_second[...].T
    second_centred[...] = centred_parts(edge_second[...])


def main_kernel(
    nodes, cotangent, edge_first, second_centred, edge_gain, node_first, node_second, node_gain, received_inner, near,
    gather_cut, gather_far, scatter_cut, scatter_far, second_t, *rest,
):
    arrived = rest[:ROUNDS]
    updated, base, grad_nodes, grad_cut = rest[ROUNDS : ROUNDS + 4]
    back = rest[ROUNDS + 4 :]
    n, width = nodes.shape
    send = arrived[0].shape[0]
    x = nodes[...]
    empty = jnp.zeros((gather_far.shape[1] - ROUNDS * send, width), bf16)
    far = jnp.concatenate([a[...] for a in arrived] + [empty], 0)
    far_end = mm(gather_far[...], far).astype(bf16)
    pre = near[...] + mm(far_end, edge_first[width : 2 * width])
    act, slope = silu_parts(pre)
    normed, inverse = norm_centred(act.astype(bf16), second_centred[...])
    received = (received_inner[...] + add_rows(scatter_cut[...], normed)) * edge_gain[...]

    pre_node = mm(jnp.concatenate([x, received.astype(bf16)], 1), node_first[...])
    act_node, slope_node = silu_parts(pre_node)
    normed_node, inverse_node = norm_centred(act_node.astype(bf16), centred_parts(node_second[...]))
    updated[...] = (x.astype(f32) + normed_node * node_gain[...]).astype(bf16)
    upstream = cotangent[...].astype(f32)
    grad_out_node = norm_backward(upstream * node_gain[...], normed_node, inverse_node).astype(bf16)
    grad_pre_node = (mm_t(grad_out_node, node_second[...]) * slope_node).astype(bf16)
    gathered = mm(gather_cut[...], grad_pre_node).astype(bf16)
    scaled = mm_t(gathered, node_first[width:]) * edge_gain[...]
    grad_out = norm_backward(scaled, normed, inverse).astype(bf16)
    grad = (mm(grad_out, second_t[...]) * slope).astype(bf16)
    sums = mm(scatter_far[...], grad).astype(bf16)
    for r in range(ROUNDS):
        back[r][...] = sums[r * send : (r + 1) * send]
    grad_cut[...] = grad
    grad_nodes[...] = grad_pre_node
    base[...] = upstream + mm_t(grad_pre_node, node_first[:width])


def outer_kernel(
    node_count, grad_nodes, node_first, edge_gain, gather, normed, inverse, slope, first_t, second_t, scatter_receive, scatter_send, scatter_cut,
    grad_cut, base, updated_in, updated, edge_gradient, cut_gradient, total,
):
    n, width = base.shape
    valid = lax.broadcasted_iota(jnp.int32, (n, width), 0) < node_count[0]
    updated[...] = jnp.where(valid, updated_in[...].astype(f32), 0.0).astype(bf16)
    cut = grad_cut[...]
    cut_gradient[...] = mm(cut, first_t[:, 2 * width :]).astype(bf16)
    gathered = mm(gather[...], grad_nodes[...]).astype(bf16)
    scaled = mm_t(gathered, node_first[width:]) * edge_gain[...]
    grad_out = norm_backward(scaled, normed[...], inverse[...]).astype(bf16)
    grad = (mm(grad_out, second_t[...]) * slope[...]).astype(bf16)
    edge_gradient[...] = mm(grad, first_t[:, 2 * width :]).astype(bf16)
    at_receiver = mm(scatter_receive[...], grad) + mm(scatter_cut[...], cut)
    at_sender = mm(scatter_send[...], grad)
    total[...] = (
        jnp.where(valid, base[...], 0.0)
        + mm(at_receiver.astype(bf16), first_t[:, :width])
        + mm(at_sender.astype(bf16), first_t[:, width : 2 * width])
    )


def last_kernel(total, scatter_boundary, first_t, updated, edge_gradient, cut_gradient, *rest):
    arrived, outs, here, done = rest[:ROUNDS], rest[ROUNDS : ROUNDS + 4], *rest[ROUNDS + 4 :]
    held = (updated, edge_gradient, cut_gradient, here)
    copies = [pltpu.make_async_copy(a, b, done.at[i]) for i, (a, b) in enumerate(zip(held, outs))]
    for copy in copies[:3]:
        copy.start()
    width = total.shape[1]
    at_sender = mm(scatter_boundary[...], jnp.concatenate([a[...] for a in arrived], 0)).astype(bf16)
    here[...] = (total[...] + mm(at_sender, first_t[:, width : 2 * width])).astype(bf16)
    copies[3].start()
    for copy in copies:
        copy.wait()


VMEM = pl.BlockSpec(memory_space=pltpu.VMEM)
HBM = pl.BlockSpec(memory_space=pltpu.HBM)
SMEM = pl.BlockSpec(memory_space=pltpu.SMEM)


def call(kernel, out_shape, args, flops, held=(), scratch=(), written=0):
    size = sum(a.size * a.dtype.itemsize for a in args + tuple(held))
    return pl.pallas_call(
        kernel,
        out_shape=out_shape,
        in_specs=[SMEM if a.ndim == 1 else VMEM for a in args] + [HBM] * len(held),
        out_specs=[VMEM if i >= written else HBM for i in range(len(out_shape))],
        scratch_shapes=scratch,
        compiler_params=pltpu.CompilerParams(vmem_limit_bytes=32 * 1024 * 1024),
        cost_estimate=pl.CostEstimate(flops=flops, bytes_accessed=size if flops else 0, transcendentals=0),
    )(*args, *(pltpu.with_memory_space_constraint(a, pltpu.HBM) for a in held))


def shards(
    node_latent, edge_latent, cut_latent, node_cotangent, edge_sender, edge_receiver, boundary_rows,
    cut_slot, cut_receiver, node_count, edge_count, edge_first, edge_second, edge_gain, node_first,
    node_second, node_gain,
):
    nodes = node_latent[0]
    edges = edge_latent[0]
    cuts = cut_latent[0].reshape(-1, cut_latent.shape[-1])
    n, width = nodes.shape
    e, c = edges.shape[0], cuts.shape[0]
    boundary = boundary_rows.transpose(1, 0, 2)
    slot = cut_slot.transpose(1, 0, 2)
    cut_targets = cut_receiver.transpose(1, 0, 2)
    send = boundary.shape[2]
    shape = jax.ShapeDtypeStruct
    kept = pltpu.VMEM

    def copies(arrays):
        return [kept(a.shape, a.dtype) for a in arrays]

    held = (boundary, nodes, edge_receiver, edge_sender, slot, cut_targets, edge_gain[None], node_gain[None])
    outs = call(
        functools.partial(send_kernel, len(held)),
        copies(held) + [kept((send, width), bf16)] * ROUNDS,
        (),
        LONG,
        held,
        [pltpu.SemaphoreType.DMA((len(held),))],
    )
    boundary, nodes, edge_receiver, edge_sender, slot, cut_targets, edge_gain, node_gain = outs[: len(held)]
    sent = outs[len(held) :]
    arrived = exchange(sent)
    slots = ROUNDS * send
    some = slots
    all_slots = -(-slots // 128) * 128
    outs = call(
        inner_kernel,
        [
            kept((e, n), bf16), kept((e, width), f32), kept((e, 1), f32), kept((e, width), f32),
            kept((n, width), f32), kept((c, width), f32), kept((c, n), bf16), kept((c, all_slots), bf16),
            kept((n, e), bf16), kept((n, e), bf16), kept((n, c), bf16), kept((some, c), bf16),
            kept((n, slots), bf16), kept((width, 3 * width), bf16), kept((width, width), bf16),
            kept((2 * width, width), bf16),
        ],
        (
            edge_count, nodes, edges, cuts, edge_sender, edge_receiver, slot, cut_targets, boundary, edge_first,
            edge_second,
        ),
        LONG,
    )
    gather, normed, inverse, slope, received, near, gather_cut, gather_far = outs[:8]
    scatter_receive, scatter_send, scatter_cut, scatter_far, scatter_boundary, first_t, second_t, second_centred = outs[8:]
    outs = call(
        main_kernel,
        [kept((n, width), bf16), kept((n, width), f32), kept((n, width), bf16), kept((c, width), bf16)]
        + [kept((send, width), bf16)] * ROUNDS,
        (
            nodes, node_cotangent[0], edge_first, second_centred, edge_gain, node_first, node_second, node_gain,
            received, near, gather_cut, gather_far, scatter_cut, scatter_far, second_t, *arrived,
        ),
        2 * c * width * width * 6,
    )
    updated, base, grad_nodes, grad_cut = outs[:4]
    returned = exchange(outs[4:])
    updated, edge_gradient, cut_gradient, total = call(
        outer_kernel,
        [kept((n, width), bf16), kept((e, width), bf16), kept((c, width), bf16), kept((n, width), f32)],
        (
            node_count, grad_nodes, node_first, edge_gain, gather, normed, inverse, slope, first_t, second_t, scatter_receive, scatter_send,
            scatter_cut, grad_cut, base, updated,
        ),
        0,
    )
    updated, edge_gradient, cut_gradient, node_gradient = call(
        last_kernel,
        [shape((n, width), bf16), shape((e, width), bf16), shape((c, width), bf16), shape((n, width), bf16)],
        (total, scatter_boundary, first_t, updated, edge_gradient, cut_gradient, *returned),
        2 * 2 * n * width * width,
        scratch=[pltpu.VMEM((n, width), bf16), pltpu.SemaphoreType.DMA((4,))],
        written=4,
    )
    return (
        updated[None],
        node_gradient[None],
        edge_gradient[None],
        cut_gradient.reshape(cut_latent.shape),
    )


def solution(mesh):
    part = ("grp", "dev")
    placed = tuple(P(part, *[None] * (d - 1)) for d in (3, 3, 4, 3, 2, 2, 3, 3, 3, 1, 1)) + (P(),) * 6
    return jax.shard_map(
        shards,
        mesh=mesh,
        in_specs=placed,
        out_specs=tuple(P(part, *[None] * (d - 1)) for d in (3, 3, 3, 4)),
        check_vma=False,
    )
```
